256 devices in a mesh: samp: 32 (over z_hi, y, core), site: 8 (over x, z_lo).
Axes of the slice: x: 4, y: 4, z: 8 (z_hi: 4, z_lo: 2; z = z_hi * 2 + z_lo), core: 2. Of those that a mesh axis runs over, the one named last changes fastest.
Arguments:
- values: bfloat16 [2048, 16384], P('samp', 'site'), may hold values from 0.099609375 to 2
- mask: int32 [2048, 16384], P('samp', 'site'), may hold values 0 or 1
- factor: float32 [2048, 128], P('samp'), may hold values from -9 to 9
Outputs:
- basis: float32 [2048, 128], P('samp')
- triangle: float32 [128, 128], replicated
The draws below stay inside these ranges and needn't reach their ends.
All inputs are finite; a program needn't handle non-finite values. No bound on the sum of `mask` on one device may be relied on, other than what follows from the above.
Results may differ from the reference program's by a relative error of at most 0.0012.
Values may be sent and summed in bfloat16 or wider, within the bound.
No kernel may reach another device: no remote copies, remote signals or barrier semaphores. Data moves between devices by JAX's collectives and lax.ppermute only.
A program may use at most 64 MiB of HBM per device.

```python
import jax
import jax.numpy as jnp
from jax import lax

SITES = 16384
K = 128
SAMPLES = 2048


def draw_factor(key, part):
    key = jax.random.fold_in(key, 7)
    keys = jax.random.split(key, 2)
    rows = jnp.arange(SAMPLES, dtype=jnp.float32)
    rising = jnp.exp(jnp.log(9.0) * rows / jnp.float32(SAMPLES - 1))
    spread = jnp.exp(jax.random.uniform(keys[0], (SAMPLES, 1), jnp.float32) * jnp.log(10.0))
    base = jax.random.uniform(keys[1], (SAMPLES, K), jnp.float32, -1.0, 1.0)
    return base * spread * rising[:, None] / 10.0


def place_ends(result, stream_key, smallest, top_value):
    place = [jax.random.randint(jax.random.fold_in(stream_key, axis), (), 0, length) for axis, length in enumerate(result.shape)]
    main_axis = result.shape.index(max(result.shape))
    beside = place[:main_axis] + [(place[main_axis] + 1) % result.shape[main_axis]] + place[main_axis + 1:]
    return result.at[tuple(place)].set(smallest).at[tuple(beside)].set(top_value)


def block_scale(key, shape, shards, smallest, top_value):
    loudness = 1.0
    for dim, parts in shards:
        draws = jax.random.uniform(jax.random.fold_in(jax.random.fold_in(key, 6), dim), (parts,), jnp.float32, smallest / len(shards), top_value / len(shards))
        loudness = loudness * jnp.repeat(jnp.exp(draws), shape[dim] // parts).reshape((-1,) + (1,) * (len(shape) - 1 - dim))
    return loudness


def setup_inputs(seed: int = 0) -> dict:
    key_of = jax.random.split(jax.random.key(seed), 4)
    return {
        "values": jnp.clip(0.099609375 + 1.9003906 * jax.random.uniform(key_of[0], (SAMPLES, SITES), jnp.float32) ** block_scale(key_of[0], (SAMPLES, SITES), ((0, 32), (1, 8)), -0.2, 0.2), 0.099609375, 2.0).astype(jnp.bfloat16),
        "mask": place_ends((jax.random.randint(key_of[1], (SAMPLES, SITES), 0, 5) < 4).astype(jnp.int32), jax.random.fold_in(key_of[1], 1), 0, 1),
        "factor": draw_factor(jax.random.fold_in(key_of[3], 71), 0),
    }


def correlate(counts, sum_row, sum_col, sq_row, sq_col, cross):
    numer = counts * cross - sum_row * sum_col
    var_row = counts * sq_row - sum_row * sum_row + counts + 1.0
    var_col = counts * sq_col - sum_col * sum_col + counts + 1.0
    return numer / jnp.sqrt(var_row * var_col)

def reference(values, mask, factor):
    held = mask.astype(jnp.bfloat16)
    masked = jnp.where(mask == 1, values, jnp.zeros_like(values))
    squares = (masked.astype(jnp.float32) * masked.astype(jnp.float32)).astype(jnp.bfloat16)
    held_f = held.astype(jnp.float32)
    masked_f = masked.astype(jnp.float32)
    squares_f = squares.astype(jnp.float32)
    counts = jnp.dot(held_f.astype(jnp.float32), held_f.T.astype(jnp.float32), preferred_element_type=jnp.float32)
    sum_row = jnp.dot(masked_f.astype(jnp.float32), held_f.T.astype(jnp.float32), preferred_element_type=jnp.float32)
    sum_col = jnp.dot(held_f.astype(jnp.float32), masked_f.T.astype(jnp.float32), preferred_element_type=jnp.float32)
    sq_row = jnp.dot(squares_f.astype(jnp.float32), held_f.T.astype(jnp.float32), preferred_element_type=jnp.float32)
    sq_col = jnp.dot(held_f.astype(jnp.float32), squares_f.T.astype(jnp.float32), preferred_element_type=jnp.float32)
    cross = jnp.dot(masked_f.astype(jnp.float32), masked_f.T.astype(jnp.float32), preferred_element_type=jnp.float32)
    band = correlate(counts, sum_row, sum_col, sq_row, sq_col, cross)
    image = jnp.dot(band, factor, precision=lax.Precision.HIGHEST)
    gram = jnp.dot(image.T, image, precision=lax.Precision.HIGHEST) / jnp.float32(SAMPLES)
    triangle = jnp.linalg.cholesky(gram)
    basis = lax.linalg.triangular_solve(triangle, image, left_side=False, lower=True, transpose_a=True)
    return (basis, triangle)
```

```python
import functools

import jax
import jax.numpy as jnp
from jax import lax
from jax.experimental import pallas as pl
from jax.experimental.pallas import tpu as pltpu
from jax.sharding import PartitionSpec as P

DEPTHS = 4
BLOCKS = 8
SITE_PARTS = 8
PANEL = 8
ROUTES = ((2, 6, 1), (6, 1, 2), (1, 2, 6))
VMEM_LIMIT = 12 * 1024 * 1024
PAIR_VMEM_LIMIT = 22 * 1024 * 1024


def correlate(counts, sum_row, sum_col, sq_row, sq_col, cross):
    numer = counts * cross - sum_row * sum_col
    var_row = counts * sq_row - sum_row * sum_row + counts + 1.0
    var_col = counts * sq_col - sum_col * sum_col + counts + 1.0
    return numer / jnp.sqrt(var_row * var_col)


def square_of(masked):
    return masked * masked


def held_of(masked):
    return jnp.minimum(masked * 16, 1)


def contract(lhs, rhs):
    return lax.dot_general(lhs, rhs, (((1,), (1,)), ((), ())), preferred_element_type=jnp.float32)


def tree_sum(parts):
    parts = list(parts)
    while len(parts) > 1:
        parts = [parts[i] + parts[i + 1] for i in range(0, len(parts), 2)]
    return parts[0]


def kernel_call(body, out_shape, scratch=(), smem=0, cost=None, limit=VMEM_LIMIT):
    params = pltpu.CompilerParams(vmem_limit_bytes=limit)

    def call(*args):
        in_specs = [pl.BlockSpec(memory_space=pltpu.SMEM)] * smem
        in_specs += [pl.BlockSpec(memory_space=pltpu.VMEM)] * (len(args) - smem)
        return pl.pallas_call(
            body,
            out_shape=out_shape,
            in_specs=in_specs,
            out_specs=jax.tree.map(lambda _: pl.BlockSpec(memory_space=pltpu.VMEM), out_shape),
            scratch_shapes=list(scratch),
            compiler_params=params,
            cost_estimate=cost,
        )(*args)

    return call


ROW_PIECES = ((0, 1), (2, 3), (6, 7), (4,), (5,))
NEAR_BLOCKS = 3


def route_offsets(route, bit):
    first, second, third = ROUTES[route]
    return [(bit * first) ^ (two * second) ^ (three * third) for two in range(2) for three in range(2)]


def pair_body(bit, chunks, which, *refs):
    n_rows = len(ROW_PIECES)
    rows = refs[:n_rows]
    cols, outs = refs[n_rows:-7], refs[-7:-4]
    stack, masked, square, held = refs[-4:]
    height = stack.shape[1]
    sites = masked.shape[1]
    for ref, slots in zip(rows, ROW_PIECES):
        for at, slot in enumerate(slots):
            stack[slot] = ref[at * height : (at + 1) * height]
    begin = 0
    for ref in cols:
        block = ref[:, :sites]
        span = slice(begin, begin + block.shape[0])
        masked[span] = block
        square[span] = square_of(block)
        held[span] = held_of(block)
        begin += block.shape[0]
    blocks = [
        jnp.concatenate([stack[which[0] ^ k] for k in route_offsets(route, bit)], axis=0) for route in range(3)
    ]
    by_held = contract(jnp.concatenate([held_of(blocks[0]), blocks[0], square_of(blocks[1])], axis=0), held[...])
    by_masked = contract(jnp.concatenate([held_of(blocks[1]), blocks[2]], axis=0), masked[...])
    by_square = contract(held_of(blocks[2]), square[...])
    count = 4 * height
    sums = (
        (by_held[:count], by_held[count : 2 * count]),
        (by_masked[:count], by_held[2 * count :]),
        (by_square, by_masked[count:]),
    )
    for out, (first, second) in zip(outs, sums):
        at, parts = 0, []
        for chunk in chunks:
            if chunk == "near":
                at = 2 * height
                parts += [first[:, :at], second[:, :at]]
            parts.append(jnp.concatenate([first[:, at : at + height], second[:, at : at + height]], axis=1))
            at += height
        joined = parts[0] if len(parts) == 1 else jnp.concatenate(parts, axis=1)
        for k in range(4):
            out[k] = joined[k * height : (k + 1) * height]


def band_body(*refs):
    near, far, whole = refs[:3], refs[3:6], refs[6:15]
    pieces, own, out = refs[15:19], refs[19], refs[20]
    height = own.shape[0]
    edge = 2 * NEAR_BLOCKS * height
    totals = []
    for r in range(3):
        rest = tree_sum([ref[0] for ref in whole[3 * r : 3 * r + 2]]) + whole[3 * r + 2][0]
        front = near[r][0] + rest[:, :edge]
        back = far[r][0] + rest[:, edge:]
        for m in range(2):
            third = slice((4 + m) * height, (5 + m) * height)
            totals.append(
                jnp.concatenate(
                    [
                        front[:, 2 * m * height : 2 * (m + 1) * height],
                        jnp.concatenate([front[:, third], back[:, m * height : (m + 1) * height]], axis=1),
                    ],
                    axis=1,
                )
            )
    band = correlate(*totals)
    columns = own.shape[1]
    gathered = [piece[:, :columns].astype(jnp.float32) + piece[:, columns:].astype(jnp.float32) for piece in pieces]
    factor = jnp.concatenate([own[...]] + gathered, axis=0)
    out[...] = jnp.dot(band, factor, precision=lax.Precision.HIGHEST, preferred_element_type=jnp.float32)


def band_call(terms, pieces, own, shape):
    columns = own.shape[1]
    firsts = [pl.BlockSpec((1,) + term.shape[1:], lambda i: (0, 0, 0)) for term in terms]
    tails = [
        pl.BlockSpec((piece.shape[0], 2 * columns), lambda i, at=piece.shape[1] // (2 * columns) - 1: (0, at))
        for piece in pieces
    ]
    whole = pl.BlockSpec(own.shape, lambda i: (0, 0))
    return pl.pallas_call(
        band_body,
        grid=(1,),
        out_shape=shape,
        in_specs=firsts + tails + [whole],
        out_specs=whole,
        compiler_params=pltpu.CompilerParams(vmem_limit_bytes=VMEM_LIMIT),
    )(*terms, *pieces, own)


def gram_body(*refs):
    out = refs[-1]
    image = tree_sum([r[...] for r in refs[:-1]])
    gram = lax.dot_general(
        image, image, (((0,), (0,)), ((), ())), precision=lax.Precision.HIGHEST, preferred_element_type=jnp.float32
    )
    packed, diagonal = pack_gram(gram)
    half = packed.shape[0]
    out[:half] = packed
    out[half : half + PANEL] = diagonal
    out[half + PANEL :] = image


def pack_gram(gram):
    half = gram.shape[0] // 2
    rows = lax.broadcasted_iota(jnp.int32, (half, half), 0)
    cols = lax.broadcasted_iota(jnp.int32, (half, half), 1)
    first = jnp.where(cols < rows, gram[half:, half:], gram[:half, :half])
    lane = lax.broadcasted_iota(jnp.int32, (half, 2 * half), 1)
    row = lax.broadcasted_iota(jnp.int32, (half, 2 * half), 0)
    diagonal = jnp.sum(jnp.where(lane == row + half, gram[half:], 0.0), axis=0, keepdims=True)
    return jnp.concatenate([first, gram[:half, half:]], axis=1), jnp.broadcast_to(diagonal, (PANEL, 2 * half))


def unpack_gram(packed, diagonal):
    half = packed.shape[0]
    lane = lax.broadcasted_iota(jnp.int32, (half, 2 * half), 1)
    row = lax.broadcasted_iota(jnp.int32, (half, 2 * half), 0) + half
    turned = packed[:, :half].T
    turned = jnp.concatenate([turned, turned], axis=1)
    return packed, jnp.where(lane == row, diagonal, turned)


def factor_body(scale, *refs):
    grams, (image_ref, basis_ref, triangle_ref, work) = refs[:2], refs[2:]
    size = work.shape[0]
    half = size // 2
    total = tree_sum([gram[...] for gram in grams]) * scale
    top, bottom = unpack_gram(total[:half], total[half : half + 1])
    rows = lax.broadcasted_iota(jnp.int32, (size, size), 0)
    cols = lax.broadcasted_iota(jnp.int32, (size, size), 1)
    shape = (PANEL, size)
    lane = lax.broadcasted_iota(jnp.int32, shape, 1)
    line = lax.broadcasted_iota(jnp.int32, shape, 0)
    count = size // PANEL
    per_half = count // 2
    left_tiles = [
        (top if t < per_half else bottom)[(t % per_half) * PANEL : (t % per_half + 1) * PANEL] for t in range(count)
    ]
    right_tiles = [jnp.where(lane == line + t * PANEL, 1.0, 0.0) for t in range(count)]

    def spread_row(tile, i):
        return jnp.broadcast_to(tile[i : i + 1], shape)

    def spread_lane(row, at):
        return jnp.broadcast_to(row[:, at : at + 1], shape)

    def gather_rows(lines):
        tile = lines[0]
        for i in range(1, PANEL):
            tile = jnp.where(line == i, lines[i], tile)
        return tile

    left = [spread_row(left_tiles[0], i) for i in range(PANEL)]
    right = [spread_row(right_tiles[0], i) for i in range(PANEL)]
    for p in range(count):
        start, following = p * PANEL, (p + 1) * PANEL
        pivot = {(i, j): spread_lane(left[i], start + j) for i in range(PANEL) for j in range(i, PANEL)}
        if p + 1 < count:
            next_left = [spread_row(left_tiles[p + 1], i) for i in range(PANEL)]
            next_right = [spread_row(right_tiles[p + 1], i) for i in range(PANEL)]
        for k in range(PANEL):
            inverse = lax.rsqrt(pivot[k, k])
            left[k] = left[k] * inverse
            right[k] = right[k] * inverse
            upper = {j: pivot[k, j] * inverse for j in range(k + 1, PANEL)}
            for i in range(k + 1, PANEL):
                left[i] = left[i] - upper[i] * left[k]
                right[i] = right[i] - upper[i] * right[k]
                for j in range(i, PANEL):
                    pivot[i, j] = pivot[i, j] - upper[i] * upper[j]
            if p + 1 < count:
                for i in range(PANEL):
                    factor = spread_lane(left[k], following + i)
                    next_left[i] = next_left[i] - factor * left[k]
                    next_right[i] = next_right[i] - factor * right[k]
        left_panel, right_panel = gather_rows(left), gather_rows(right)
        work[start:following, :size] = left_panel
        work[start:following, size:] = right_panel
        if p + 2 < count:
            update = lax.dot_general(
                left_panel, jnp.concatenate([left_panel, right_panel], axis=1), (((0,), (0,)), ((), ())),
                precision=lax.Precision.HIGHEST, preferred_element_type=jnp.float32,
            )
            for t in range(p + 2, count):
                span = slice(t * PANEL, (t + 1) * PANEL)
                left_tiles[t] = left_tiles[t] - update[span, :size]
                right_tiles[t] = right_tiles[t] - update[span, size:]
        if p + 1 < count:
            left, right = next_left, next_right
    upper = jnp.where(cols >= rows, work[:, :size], 0.0)
    triangle_ref[...] = upper.T
    basis_ref[...] = lax.dot_general(
        image_ref[...], work[:, size:], (((1,), (1,)), ((), ())),
        precision=lax.Precision.HIGHEST, preferred_element_type=jnp.float32,
    )


def samp_perm(shift):
    return [(i, i ^ shift) for i in range(DEPTHS * BLOCKS)]


def site_perm(shift):
    return [(i, i ^ shift) for i in range(SITE_PARTS)]


def gather_line(block, near, other):
    half = block.shape[0] // 2
    one = lax.ppermute(block, "samp", samp_perm(near))
    three = lax.ppermute(block, "samp", samp_perm(other))
    top = lax.ppermute(one[:half], "samp", samp_perm(other))
    bottom = lax.ppermute(three[half:], "samp", samp_perm(near))
    return [block, one, three, top, bottom]


def spread(part, axis, shifts):
    perm = samp_perm if axis == "samp" else site_perm
    return [part] + [lax.ppermute(part, axis, perm(k)) for k in shifts]


def local(values, mask, factor):
    height, sites = values.shape
    columns = factor.shape[1]
    f32 = jnp.float32
    masked = jnp.where(mask == 1, values, jnp.zeros_like(values))
    rounded = lax.reduce_precision(factor, 8, 7)
    coarse, fine = rounded.astype(jnp.bfloat16), (factor - rounded).astype(jnp.bfloat16)
    tagged = jnp.concatenate([masked, coarse, fine], axis=1)
    both = jnp.concatenate([masked, lax.ppermute(masked, "samp", samp_perm(1))], axis=0)
    rows = gather_line(both, 2, 6)
    pieces = gather_line(tagged, BLOCKS, 3 * BLOCKS)[1:]
    near_cols, far_cols = [masked] + pieces[:2], pieces[2:]
    which = ((lax.axis_index("samp") % BLOCKS) ^ lax.axis_index("site")).astype(jnp.int32).reshape(1)

    def pairs(bit, chunks, cols, flops):
        lanes = {"near": 2 * NEAR_BLOCKS * height, "far": 2 * height}
        width = sum(col.shape[0] for col in cols)
        return kernel_call(
            functools.partial(pair_body, bit, chunks),
            [jax.ShapeDtypeStruct((4, height, sum(lanes[chunk] for chunk in chunks)), f32)] * 3,
            scratch=[pltpu.VMEM((BLOCKS, height, sites), jnp.bfloat16)] + [pltpu.VMEM((width, sites), jnp.bfloat16)] * 3,
            smem=1,
            limit=PAIR_VMEM_LIMIT,
            cost=pl.CostEstimate(flops=flops, bytes_accessed=100000, transcendentals=0),
        )(which, *rows, *cols)

    send_near = pairs(1, ("near",), near_cols, 1000000)
    came_near = [lax.ppermute(send_near[r], "site", site_perm(ROUTES[r][0])) for r in range(3)]
    far_cols[0], _ = lax.optimization_barrier((far_cols[0], send_near))
    send_far = pairs(1, ("far",), far_cols, 10000000000)
    came_far = [lax.ppermute(send_far[r], "site", site_perm(ROUTES[r][0])) for r in range(3)]
    far_kept, came_near, _ = lax.optimization_barrier((far_cols[1], came_near, send_far))
    keep = pairs(0, ("near", "far"), near_cols + [far_cols[0], far_kept], 10000000000)
    keep, came_far = lax.optimization_barrier((keep, came_far))

    def arrived(r, at):
        return jnp.concatenate([came_near[r][at], came_far[r][at]], axis=2)

    send = [keep[r][2:] + arrived(r, slice(2, 4)) for r in range(3)]
    came2 = [lax.ppermute(send[r], "site", site_perm(ROUTES[r][1])) for r in range(3)]
    send = [(keep[r][1:2] + came2[r][1:2]) + arrived(r, slice(1, 2)) for r in range(3)]
    came3 = [lax.ppermute(send[r], "site", site_perm(ROUTES[r][2])) for r in range(3)]
    terms = came_near + came_far + [t for r in range(3) for t in (keep[r], came2[r], came3[r])]
    part = band_call(terms, pieces, factor, jax.ShapeDtypeStruct((height, columns), f32))
    part = tree_sum(spread(part, "samp", [1]))
    packed = columns // 2 + PANEL
    message = kernel_call(gram_body, jax.ShapeDtypeStruct((packed + height, columns), f32))(*spread(part, "samp", [2, 4, 6]))
    is_gram = lax.broadcasted_iota(jnp.int32, message.shape, 0) < packed
    apart = which[0]
    came = spread(message, "site", [2, 4, 6])
    turn = apart >> 1
    picked = jnp.where(turn < 2, jnp.where(turn == 0, came[0], came[1]), jnp.where(turn == 2, came[2], came[3]))
    message = jnp.where(is_gram, tree_sum(came), picked)
    came = spread(message, "site", [1])
    message = jnp.where(is_gram, tree_sum(came), jnp.where((apart & 1) == 0, came[0], came[1]))
    gram, own_image = message[:packed], message[packed:]
    gram = tree_sum(spread(gram, "samp", [BLOCKS]))
    grams = spread(gram, "samp", [3 * BLOCKS])
    scale = 1.0 / (height * DEPTHS * BLOCKS)
    basis, triangle = kernel_call(
        functools.partial(factor_body, scale),
        [jax.ShapeDtypeStruct((height, columns), f32), jax.ShapeDtypeStruct((columns, columns), f32)],
        scratch=[pltpu.VMEM((columns, 2 * columns), f32)],
    )(*grams, own_image)
    return (basis, triangle)


def solution(mesh):
    return jax.shard_map(
        local,
        mesh=mesh,
        in_specs=(P("samp", "site"), P("samp", "site"), P("samp", None)),
        out_specs=(P("samp", None), P()),
        check_vma=False,
    )
```

```python
import functools

import jax
import jax.numpy as jnp
from jax import lax
from jax.experimental import pallas as pl
from jax.experimental.pallas import tpu as pltpu
from jax.sharding import PartitionSpec as P

DEPTHS = 4
BLOCKS = 8
SITE_PARTS = 8
PANEL = 8
ROUTES = ((2, 6, 1), (6, 1, 2), (1, 2, 6))
VMEM_LIMIT = 12 * 1024 * 1024
PAIR_VMEM_LIMIT = 22 * 1024 * 1024


def correlate(counts, sum_row, sum_col, sq_row, sq_col, cross):
    numer = counts * cross - sum_row * sum_col
    var_row = counts * sq_row - sum_row * sum_row + counts + 1.0
    var_col = counts * sq_col - sum_col * sum_col + counts + 1.0
    return numer / jnp.sqrt(var_row * var_col)


def square_of(masked):
    return masked * masked


def held_of(masked):
    return jnp.minimum(masked * 16, 1)


def contract(lhs, rhs):
    return lax.dot_general(lhs, rhs, (((1,), (1,)), ((), ())), preferred_element_type=jnp.float32)


def tree_sum(parts):
    parts = list(parts)
    while len(parts) > 1:
        parts = [parts[i] + parts[i + 1] for i in range(0, len(parts), 2)]
    return parts[0]


def kernel_call(body, out_shape, scratch=(), smem=0, cost=None, limit=VMEM_LIMIT):
    params = pltpu.CompilerParams(vmem_limit_bytes=limit)

    def call(*args):
        in_specs = [pl.BlockSpec(memory_space=pltpu.SMEM)] * smem
        in_specs += [pl.BlockSpec(memory_space=pltpu.VMEM)] * (len(args) - smem)
        return pl.pallas_call(
            body,
            out_shape=out_shape,
            in_specs=in_specs,
            out_specs=jax.tree.map(lambda _: pl.BlockSpec(memory_space=pltpu.VMEM), out_shape),
            scratch_shapes=list(scratch),
            compiler_params=params,
            cost_estimate=cost,
        )(*args)

    return call


ROW_PIECES = ((0, 1), (2, 3), (6, 7), (4,), (5,))
NEAR_BLOCKS = 3


def route_offsets(route, bit):
    first, second, third = ROUTES[route]
    return [(bit * first) ^ (two * second) ^ (three * third) for two in range(2) for three in range(2)]


def pair_body(bit, chunks, which, *refs):
    n_rows = len(ROW_PIECES)
    rows = refs[:n_rows]
    cols, outs = refs[n_rows:-7], refs[-7:-4]
    stack, masked, square, held = refs[-4:]
    height = stack.shape[1]
    sites = masked.shape[1]
    for ref, slots in zip(rows, ROW_PIECES):
        for at, slot in enumerate(slots):
            stack[slot] = ref[at * height : (at + 1) * height]
    begin = 0
    for ref in cols:
        block = ref[:, :sites]
        span = slice(begin, begin + block.shape[0])
        masked[span] = block
        square[span] = square_of(block)
        held[span] = held_of(block)
        begin += block.shape[0]
    blocks = [
        jnp.concatenate([stack[which[0] ^ k] for k in route_offsets(route, bit)], axis=0) for route in range(3)
    ]
    by_held = contract(jnp.concatenate([held_of(blocks[0]), blocks[0], square_of(blocks[1])], axis=0), held[...])
    by_masked = contract(jnp.concatenate([held_of(blocks[1]), blocks[2]], axis=0), masked[...])
    by_square = contract(held_of(blocks[2]), square[...])
    count = 4 * height
    sums = (
        (by_held[:count], by_held[count : 2 * count]),
        (by_masked[:count], by_held[2 * count :]),
        (by_square, by_masked[count:]),
    )
    for out, (first, second) in zip(outs, sums):
        at, parts = 0, []
        for chunk in chunks:
            if chunk == "near":
                at = 2 * height
                parts += [first[:, :at], second[:, :at]]
            parts.append(jnp.concatenate([first[:, at : at + height], second[:, at : at + height]], axis=1))
            at += height
        joined = parts[0] if len(parts) == 1 else jnp.concatenate(parts, axis=1)
        for k in range(4):
            out[k] = joined[k * height : (k + 1) * height]


def fold_body(keep, near, far, send, later, last):
    edge = near.shape[2]
    for out, begin in ((send, 2), (later, 1), (last, 0)):
        span = slice(begin, begin + out.shape[0])
        out[:, :, :edge] = keep[span, :, :edge] + near[span]
        out[:, :, edge:] = keep[span, :, edge:] + far[span]


def fold(keep, near, far):
    shapes = [jax.ShapeDtypeStruct((count,) + keep.shape[1:], jnp.float32) for count in (2, 1, 1)]
    return kernel_call(fold_body, shapes)(keep, near, far)


def band_body(*refs):
    whole, pieces, own, out = refs[:9], refs[9:13], refs[13], refs[14]
    height = own.shape[0]
    edge = 2 * NEAR_BLOCKS * height
    totals = []
    for r in range(3):
        rest = (whole[3 * r][0] + whole[3 * r + 1][0]) + whole[3 * r + 2][0]
        front, back = rest[:, :edge], rest[:, edge:]
        for m in range(2):
            third = slice((4 + m) * height, (5 + m) * height)
            totals.append(
                jnp.concatenate(
                    [
                        front[:, 2 * m * height : 2 * (m + 1) * height],
                        jnp.concatenate([front[:, third], back[:, m * height : (m + 1) * height]], axis=1),
                    ],
                    axis=1,
                )
            )
    band = correlate(*totals)
    columns = own.shape[1]
    gathered = [piece[:, :columns].astype(jnp.float32) + piece[:, columns:].astype(jnp.float32) for piece in pieces]
    factor = jnp.concatenate([own[...]] + gathered, axis=0)
    out[...] = jnp.dot(band, factor, precision=lax.Precision.HIGHEST, preferred_element_type=jnp.float32)


def band_call(terms, pieces, own, shape):
    columns = own.shape[1]
    firsts = [pl.BlockSpec((1,) + term.shape[1:], lambda i: (0, 0, 0)) for term in terms]
    tails = [
        pl.BlockSpec((piece.shape[0], 2 * columns), lambda i, at=piece.shape[1] // (2 * columns) - 1: (0, at))
        for piece in pieces
    ]
    whole = pl.BlockSpec(own.shape, lambda i: (0, 0))
    return pl.pallas_call(
        band_body,
        grid=(1,),
        out_shape=shape,
        in_specs=firsts + tails + [whole],
        out_specs=whole,
        compiler_params=pltpu.CompilerParams(vmem_limit_bytes=VMEM_LIMIT),
    )(*terms, *pieces, own)


def gram_body(*refs):
    out = refs[-1]
    image = tree_sum([r[...] for r in refs[:-1]])
    gram = lax.dot_general(
        image, image, (((0,), (0,)), ((), ())), precision=lax.Precision.HIGHEST, preferred_element_type=jnp.float32
    )
    packed, diagonal = pack_gram(gram)
    half = packed.shape[0]
    out[:half] = packed
    out[half : half + PANEL] = diagonal
    out[half + PANEL :] = image


def pack_gram(gram):
    half = gram.shape[0] // 2
    rows = lax.broadcasted_iota(jnp.int32, (half, half), 0)
    cols = lax.broadcasted_iota(jnp.int32, (half, half), 1)
    first = jnp.where(cols < rows, gram[half:, half:], gram[:half, :half])
    lane = lax.broadcasted_iota(jnp.int32, (half, 2 * half), 1)
    row = lax.broadcasted_iota(jnp.int32, (half, 2 * half), 0)
    diagonal = jnp.sum(jnp.where(lane == row + half, gram[half:], 0.0), axis=0, keepdims=True)
    return jnp.concatenate([first, gram[:half, half:]], axis=1), jnp.broadcast_to(diagonal, (PANEL, 2 * half))


def unpack_gram(packed, diagonal):
    half = packed.shape[0]
    lane = lax.broadcasted_iota(jnp.int32, (half, 2 * half), 1)
    row = lax.broadcasted_iota(jnp.int32, (half, 2 * half), 0) + half
    turned = packed[:, :half].T
    turned = jnp.concatenate([turned, turned], axis=1)
    return packed, jnp.where(lane == row, diagonal, turned)


def factor_body(scale, *refs):
    grams, (image_ref, basis_ref, triangle_ref, work) = refs[:2], refs[2:]
    size = work.shape[0]
    half = size // 2
    total = tree_sum([gram[...] for gram in grams]) * scale
    top, bottom = unpack_gram(total[:half], total[half : half + 1])
    rows = lax.broadcasted_iota(jnp.int32, (size, size), 0)
    cols = lax.broadcasted_iota(jnp.int32, (size, size), 1)
    shape = (PANEL, size)
    lane = lax.broadcasted_iota(jnp.int32, shape, 1)
    line = lax.broadcasted_iota(jnp.int32, shape, 0)
    count = size // PANEL
    per_half = count // 2
    left_tiles = [
        (top if t < per_half else bottom)[(t % per_half) * PANEL : (t % per_half + 1) * PANEL] for t in range(count)
    ]
    right_tiles = [jnp.where(lane == line + t * PANEL, 1.0, 0.0) for t in range(count)]

    def spread_row(tile, i):
        return jnp.broadcast_to(tile[i : i + 1], shape)

    def spread_lane(row, at):
        return jnp.broadcast_to(row[:, at : at + 1], shape)

    def gather_rows(lines):
        tile = lines[0]
        for i in range(1, PANEL):
            tile = jnp.where(line == i, lines[i], tile)
        return tile

    left = [spread_row(left_tiles[0], i) for i in range(PANEL)]
    right = [spread_row(right_tiles[0], i) for i in range(PANEL)]
    for p in range(count):
        start, following = p * PANEL, (p + 1) * PANEL
        pivot = {(i, j): spread_lane(left[i], start + j) for i in range(PANEL) for j in range(i, PANEL)}
        if p + 1 < count:
            next_left = [spread_row(left_tiles[p + 1], i) for i in range(PANEL)]
            next_right = [spread_row(right_tiles[p + 1], i) for i in range(PANEL)]
        for k in range(PANEL):
            inverse = lax.rsqrt(pivot[k, k])
            left[k] = left[k] * inverse
            right[k] = right[k] * inverse
            upper = {j: pivot[k, j] * inverse for j in range(k + 1, PANEL)}
            for i in range(k + 1, PANEL):
                left[i] = left[i] - upper[i] * left[k]
                right[i] = right[i] - upper[i] * right[k]
                for j in range(i, PANEL):
                    pivot[i, j] = pivot[i, j] - upper[i] * upper[j]
            if p + 1 < count:
                for i in range(PANEL):
                    factor = spread_lane(left[k], following + i)
                    next_left[i] = next_left[i] - factor * left[k]
                    next_right[i] = next_right[i] - factor * right[k]
        left_panel, right_panel = gather_rows(left), gather_rows(right)
        work[start:following, :size] = left_panel
        work[start:following, size:] = right_panel
        if p + 2 < count:
            update = lax.dot_general(
                left_panel, jnp.concatenate([left_panel, right_panel], axis=1), (((0,), (0,)), ((), ())),
                precision=lax.Precision.HIGHEST, preferred_element_type=jnp.float32,
            )
            for t in range(p + 2, count):
                span = slice(t * PANEL, (t + 1) * PANEL)
                left_tiles[t] = left_tiles[t] - update[span, :size]
                right_tiles[t] = right_tiles[t] - update[span, size:]
        if p + 1 < count:
            left, right = next_left, next_right
    upper = jnp.where(cols >= rows, work[:, :size], 0.0)
    triangle_ref[...] = upper.T
    basis_ref[...] = lax.dot_general(
        image_ref[...], work[:, size:], (((1,), (1,)), ((), ())),
        precision=lax.Precision.HIGHEST, preferred_element_type=jnp.float32,
    )


def samp_perm(shift):
    return [(i, i ^ shift) for i in range(DEPTHS * BLOCKS)]


def site_perm(shift):
    return [(i, i ^ shift) for i in range(SITE_PARTS)]


def half_body(whole, out):
    out[...] = whole[...]


def half_of(block, part):
    shape = (block.shape[0] // 2, block.shape[1])
    return pl.pallas_call(
        half_body,
        grid=(1,),
        out_shape=jax.ShapeDtypeStruct(shape, block.dtype),
        in_specs=[pl.BlockSpec(shape, lambda i: (part, 0))],
        out_specs=pl.BlockSpec(shape, lambda i: (0, 0)),
        compiler_params=pltpu.CompilerParams(vmem_limit_bytes=VMEM_LIMIT),
    )(block)


def gather_line(block, near, other):
    one = lax.ppermute(block, "samp", samp_perm(near))
    three = lax.ppermute(block, "samp", samp_perm(other))
    top = lax.ppermute(half_of(one, 0), "samp", samp_perm(other))
    bottom = lax.ppermute(half_of(three, 1), "samp", samp_perm(near))
    return [block, one, three, top, bottom]


def spread(part, axis, shifts):
    perm = samp_perm if axis == "samp" else site_perm
    return [part] + [lax.ppermute(part, axis, perm(k)) for k in shifts]


def local(values, mask, factor):
    height, sites = values.shape
    columns = factor.shape[1]
    f32 = jnp.float32
    masked = jnp.where(mask == 1, values, jnp.zeros_like(values))
    rounded = lax.reduce_precision(factor, 8, 7)
    coarse, fine = rounded.astype(jnp.bfloat16), (factor - rounded).astype(jnp.bfloat16)
    tagged = jnp.concatenate([masked, coarse, fine], axis=1)
    both = jnp.concatenate([masked, lax.ppermute(masked, "samp", samp_perm(1))], axis=0)
    rows = gather_line(both, 2, 6)
    pieces = gather_line(tagged, BLOCKS, 3 * BLOCKS)[1:]
    near_cols, far_cols = [masked] + pieces[:2], pieces[2:]
    which = ((lax.axis_index("samp") % BLOCKS) ^ lax.axis_index("site")).astype(jnp.int32).reshape(1)

    def pairs(bit, chunks, cols, flops):
        lanes = {"near": 2 * NEAR_BLOCKS * height, "far": 2 * height}
        width = sum(col.shape[0] for col in cols)
        return kernel_call(
            functools.partial(pair_body, bit, chunks),
            [jax.ShapeDtypeStruct((4, height, sum(lanes[chunk] for chunk in chunks)), f32)] * 3,
            scratch=[pltpu.VMEM((BLOCKS, height, sites), jnp.bfloat16)] + [pltpu.VMEM((width, sites), jnp.bfloat16)] * 3,
            smem=1,
            limit=PAIR_VMEM_LIMIT,
            cost=pl.CostEstimate(flops=flops, bytes_accessed=100000, transcendentals=0),
        )(which, *rows, *cols)

    send_near = pairs(1, ("near",), near_cols, 1000000)
    came_near = [lax.ppermute(send_near[r], "site", site_perm(ROUTES[r][0])) for r in range(3)]
    far_cols[0], _ = lax.optimization_barrier((far_cols[0], send_near))
    send_far = pairs(1, ("far",), far_cols, 10000000000)
    came_far = [lax.ppermute(send_far[r], "site", site_perm(ROUTES[r][0])) for r in range(3)]
    far_kept, came_near, _ = lax.optimization_barrier((far_cols[1], came_near, send_far))
    keep = pairs(0, ("near", "far"), near_cols + [far_cols[0], far_kept], 10000000000)
    keep, came_far = lax.optimization_barrier((keep, came_far))
    folded = [fold(keep[r], came_near[r], came_far[r]) for r in range(3)]
    came2 = [lax.ppermute(folded[r][0], "site", site_perm(ROUTES[r][1])) for r in range(3)]
    send = [folded[r][1] + came2[r][1:] for r in range(3)]
    came3 = [lax.ppermute(send[r], "site", site_perm(ROUTES[r][2])) for r in range(3)]
    terms = [t for r in range(3) for t in (folded[r][2], came2[r], came3[r])]
    part = band_call(terms, pieces, factor, jax.ShapeDtypeStruct((height, columns), f32))
    part = tree_sum(spread(part, "samp", [1]))
    packed = columns // 2 + PANEL
    message = kernel_call(gram_body, jax.ShapeDtypeStruct((packed + height, columns), f32))(*spread(part, "samp", [2, 4, 6]))
    is_gram = lax.broadcasted_iota(jnp.int32, message.shape, 0) < packed
    apart = which[0]
    came = spread(message, "site", [2, 4, 6])
    turn = apart >> 1
    picked = jnp.where(turn < 2, jnp.where(turn == 0, came[0], came[1]), jnp.where(turn == 2, came[2], came[3]))
    message = jnp.where(is_gram, tree_sum(came), picked)
    came = spread(message, "site", [1])
    message = jnp.where(is_gram, tree_sum(came), jnp.where((apart & 1) == 0, came[0], came[1]))
    gram, own_image = message[:packed], message[packed:]
    gram = tree_sum(spread(gram, "samp", [BLOCKS]))
    grams = spread(gram, "samp", [3 * BLOCKS])
    scale = 1.0 / (height * DEPTHS * BLOCKS)
    basis, triangle = kernel_call(
        functools.partial(factor_body, scale),
        [jax.ShapeDtypeStruct((height, columns), f32), jax.ShapeDtypeStruct((columns, columns), f32)],
        scratch=[pltpu.VMEM((columns, 2 * columns), f32)],
    )(*grams, own_image)
    return (basis, triangle)


def solution(mesh):
    return jax.shard_map(
        local,
        mesh=mesh,
        in_specs=(P("samp", "site"), P("samp", "site"), P("samp", None)),
        out_specs=(P("samp", None), P()),
        check_vma=False,
    )
```

```python
import functools

import jax
import jax.numpy as jnp
from jax import lax
from jax.experimental import pallas as pl
from jax.experimental.pallas import tpu as pltpu
from jax.sharding import PartitionSpec as P

DEPTHS = 4
BLOCKS = 8
SITE_PARTS = 8
PANEL = 8
ROUTES = ((2, 6, 1), (6, 1, 2), (1, 2, 6))
VMEM_LIMIT = 12 * 1024 * 1024
PAIR_VMEM_LIMIT = 22 * 1024 * 1024


def correlate(counts, sum_row, sum_col, sq_row, sq_col, cross):
    numer = counts * cross - sum_row * sum_col
    var_row = counts * sq_row - sum_row * sum_row + counts + 1.0
    var_col = counts * sq_col - sum_col * sum_col + counts + 1.0
    return numer / jnp.sqrt(var_row * var_col)


def square_of(masked):
    return masked * masked


def held_of(masked):
    return jnp.minimum(masked * 16, 1)


def contract(lhs, rhs):
    return lax.dot_general(lhs, rhs, (((1,), (1,)), ((), ())), preferred_element_type=jnp.float32)


def tree_sum(parts):
    parts = list(parts)
    while len(parts) > 1:
        parts = [parts[i] + parts[i + 1] for i in range(0, len(parts), 2)]
    return parts[0]


def kernel_call(body, out_shape, scratch=(), smem=0, cost=None, limit=VMEM_LIMIT):
    params = pltpu.CompilerParams(vmem_limit_bytes=limit)

    def call(*args):
        in_specs = [pl.BlockSpec(memory_space=pltpu.SMEM)] * smem
        in_specs += [pl.BlockSpec(memory_space=pltpu.VMEM)] * (len(args) - smem)
        return pl.pallas_call(
            body,
            out_shape=out_shape,
            in_specs=in_specs,
            out_specs=jax.tree.map(lambda _: pl.BlockSpec(memory_space=pltpu.VMEM), out_shape),
            scratch_shapes=list(scratch),
            compiler_params=params,
            cost_estimate=cost,
        )(*args)

    return call


ROW_PIECES = ((0,), (2, 6), (4,), (1,), (3, 7), (5,))
NEAR_BLOCKS = 3


def route_offsets(route, bit):
    first, second, third = ROUTES[route]
    return [(bit * first) ^ (two * second) ^ (three * third) for two in range(2) for three in range(2)]


def pair_body(bit, chunks, which, *refs):
    n_rows = len(ROW_PIECES)
    rows = refs[:n_rows]
    whole = len(chunks) == 2
    cols, outs = refs[n_rows : -7 - whole], refs[-7 - whole : -4 - whole]
    stack, masked, square, held = refs[-4:]
    height = stack.shape[1]
    sites = masked.shape[1]
    for ref, slots in zip(rows, ROW_PIECES):
        for at, slot in enumerate(slots):
            stack[slot] = ref[at * height : (at + 1) * height]
    begin = 0
    for ref in cols:
        block = ref[:, :sites]
        span = slice(begin, begin + block.shape[0])
        masked[span] = block
        square[span] = square_of(block)
        held[span] = held_of(block)
        if whole and begin > 0:
            columns = (ref.shape[1] - sites) // 2
            gathered = ref[:, sites : sites + columns].astype(jnp.float32) + ref[:, sites + columns :].astype(jnp.float32)
            refs[-5][begin - height : begin - height + block.shape[0]] = gathered
        begin += block.shape[0]
    blocks = [
        jnp.concatenate([stack[which[0] ^ k] for k in route_offsets(route, bit)], axis=0) for route in range(3)
    ]
    by_held = contract(jnp.concatenate([held_of(blocks[0]), blocks[0], square_of(blocks[1])], axis=0), held[...])
    by_masked = contract(jnp.concatenate([held_of(blocks[1]), blocks[2]], axis=0), masked[...])
    by_square = contract(held_of(blocks[2]), square[...])
    count = 4 * height
    sums = (
        (by_held[:count], by_held[count : 2 * count]),
        (by_masked[:count], by_held[2 * count :]),
        (by_square, by_masked[count:]),
    )
    for out, (first, second) in zip(outs, sums):
        at, parts = 0, []
        for chunk in chunks:
            if chunk == "near":
                at = 2 * height
                parts += [first[:, :at], second[:, :at]]
            parts.append(jnp.concatenate([first[:, at : at + height], second[:, at : at + height]], axis=1))
            at += height
        joined = parts[0] if len(parts) == 1 else jnp.concatenate(parts, axis=1)
        for k in range(4):
            out[k] = joined[k * height : (k + 1) * height]


def fold_body(keep, near, far, send, later, last):
    edge = near.shape[2]
    for out, begin in ((send, 2), (later, 1), (last, 0)):
        span = slice(begin, begin + out.shape[0])
        out[:, :, :edge] = keep[span, :, :edge] + near[span]
        out[:, :, edge:] = keep[span, :, edge:] + far[span]


def fold(keep, near, far):
    shapes = [jax.ShapeDtypeStruct((count,) + keep.shape[1:], jnp.float32) for count in (2, 1, 1)]
    return kernel_call(fold_body, shapes)(keep, near, far)


def band_body(*refs):
    whole, gathered, own, out = refs[:9], refs[9], refs[10], refs[11]
    height = own.shape[0]
    edge = 2 * NEAR_BLOCKS * height
    totals = []
    for r in range(3):
        rest = (whole[3 * r][0] + whole[3 * r + 1][0]) + whole[3 * r + 2][0]
        front, back = rest[:, :edge], rest[:, edge:]
        for m in range(2):
            third = slice((4 + m) * height, (5 + m) * height)
            totals.append(
                jnp.concatenate(
                    [
                        front[:, 2 * m * height : 2 * (m + 1) * height],
                        jnp.concatenate([front[:, third], back[:, m * height : (m + 1) * height]], axis=1),
                    ],
                    axis=1,
                )
            )
    band = correlate(*totals)
    factor = jnp.concatenate([own[...], gathered[...]], axis=0)
    out[...] = jnp.dot(band, factor, precision=lax.Precision.HIGHEST, preferred_element_type=jnp.float32)


def gram_body(*refs):
    out = refs[-1]
    image = tree_sum([r[...] for r in refs[:-1]])
    gram = lax.dot_general(
        image, image, (((0,), (0,)), ((), ())), precision=lax.Precision.HIGHEST, preferred_element_type=jnp.float32
    )
    packed, diagonal = pack_gram(gram)
    half = packed.shape[0]
    out[:half] = packed
    out[half : half + PANEL] = diagonal
    out[half + PANEL :] = image


def pack_gram(gram):
    half = gram.shape[0] // 2
    rows = lax.broadcasted_iota(jnp.int32, (half, half), 0)
    cols = lax.broadcasted_iota(jnp.int32, (half, half), 1)
    first = jnp.where(cols < rows, gram[half:, half:], gram[:half, :half])
    lane = lax.broadcasted_iota(jnp.int32, (half, 2 * half), 1)
    row = lax.broadcasted_iota(jnp.int32, (half, 2 * half), 0)
    diagonal = jnp.sum(jnp.where(lane == row + half, gram[half:], 0.0), axis=0, keepdims=True)
    return jnp.concatenate([first, gram[:half, half:]], axis=1), jnp.broadcast_to(diagonal, (PANEL, 2 * half))


def unpack_gram(packed, diagonal):
    half = packed.shape[0]
    lane = lax.broadcasted_iota(jnp.int32, (half, 2 * half), 1)
    row = lax.broadcasted_iota(jnp.int32, (half, 2 * half), 0) + half
    turned = packed[:, :half].T
    turned = jnp.concatenate([turned, turned], axis=1)
    return packed, jnp.where(lane == row, diagonal, turned)


def factor_body(scale, *refs):
    grams, (image_ref, basis_ref, triangle_ref, work) = refs[:2], refs[2:]
    size = work.shape[0]
    half = size // 2
    total = tree_sum([gram[...] for gram in grams]) * scale
    top, bottom = unpack_gram(total[:half], total[half : half + 1])
    rows = lax.broadcasted_iota(jnp.int32, (size, size), 0)
    cols = lax.broadcasted_iota(jnp.int32, (size, size), 1)
    shape = (PANEL, size)
    lane = lax.broadcasted_iota(jnp.int32, shape, 1)
    line = lax.broadcasted_iota(jnp.int32, shape, 0)
    count = size // PANEL
    per_half = count // 2
    left_tiles = [
        (top if t < per_half else bottom)[(t % per_half) * PANEL : (t % per_half + 1) * PANEL] for t in range(count)
    ]
    right_tiles = [jnp.where(lane == line + t * PANEL, 1.0, 0.0) for t in range(count)]

    def spread_row(tile, i):
        return jnp.broadcast_to(tile[i : i + 1], shape)

    def spread_lane(row, at):
        return jnp.broadcast_to(row[:, at : at + 1], shape)

    def gather_rows(lines):
        tile = lines[0]
        for i in range(1, PANEL):
            tile = jnp.where(line == i, lines[i], tile)
        return tile

    left = [spread_row(left_tiles[0], i) for i in range(PANEL)]
    right = [spread_row(right_tiles[0], i) for i in range(PANEL)]
    for p in range(count):
        start, following = p * PANEL, (p + 1) * PANEL
        pivot = {(i, j): spread_lane(left[i], start + j) for i in range(PANEL) for j in range(i, PANEL)}
        if p + 1 < count:
            next_left = [spread_row(left_tiles[p + 1], i) for i in range(PANEL)]
            next_right = [spread_row(right_tiles[p + 1], i) for i in range(PANEL)]
        for k in range(PANEL):
            inverse = lax.rsqrt(pivot[k, k])
            left[k] = left[k] * inverse
            right[k] = right[k] * inverse
            upper = {j: pivot[k, j] * inverse for j in range(k + 1, PANEL)}
            for i in range(k + 1, PANEL):
                left[i] = left[i] - upper[i] * left[k]
                right[i] = right[i] - upper[i] * right[k]
                for j in range(i, PANEL):
                    pivot[i, j] = pivot[i, j] - upper[i] * upper[j]
            if p + 1 < count:
                for i in range(PANEL):
                    factor = spread_lane(left[k], following + i)
                    next_left[i] = next_left[i] - factor * left[k]
                    next_right[i] = next_right[i] - factor * right[k]
        left_panel, right_panel = gather_rows(left), gather_rows(right)
        work[start:following, :size] = left_panel
        work[start:following, size:] = right_panel
        if p + 2 < count:
            update = lax.dot_general(
                left_panel, jnp.concatenate([left_panel, right_panel], axis=1), (((0,), (0,)), ((), ())),
                precision=lax.Precision.HIGHEST, preferred_element_type=jnp.float32,
            )
            for t in range(p + 2, count):
                span = slice(t * PANEL, (t + 1) * PANEL)
                left_tiles[t] = left_tiles[t] - update[span, :size]
                right_tiles[t] = right_tiles[t] - update[span, size:]
        if p + 1 < count:
            left, right = next_left, next_right
    upper = jnp.where(cols >= rows, work[:, :size], 0.0)
    triangle_ref[...] = upper.T
    basis_ref[...] = lax.dot_general(
        image_ref[...], work[:, size:], (((1,), (1,)), ((), ())),
        precision=lax.Precision.HIGHEST, preferred_element_type=jnp.float32,
    )


def samp_perm(shift):
    return [(i, i ^ shift) for i in range(DEPTHS * BLOCKS)]


def site_perm(shift):
    return [(i, i ^ shift) for i in range(SITE_PARTS)]


def half_body(part, whole, out):
    count = out.shape[0]
    out[...] = whole[part * count : (part + 1) * count]


def half_of(block, part):
    shape = jax.ShapeDtypeStruct((block.shape[0] // 2, block.shape[1]), block.dtype)
    return kernel_call(functools.partial(half_body, part), shape)(block)


def gather_line(block, near, other, cut):
    one = lax.ppermute(block, "samp", samp_perm(near))
    three = lax.ppermute(block, "samp", samp_perm(other))
    top = lax.ppermute(cut(one, 0), "samp", samp_perm(other))
    bottom = lax.ppermute(cut(three, 1), "samp", samp_perm(near))
    return [block, one, three, top, bottom]


def spread(part, axis, shifts):
    perm = samp_perm if axis == "samp" else site_perm
    return [part] + [lax.ppermute(part, axis, perm(k)) for k in shifts]


def local(values, mask, factor):
    height, sites = values.shape
    columns = factor.shape[1]
    f32 = jnp.float32
    masked = jnp.where(mask == 1, values, jnp.zeros_like(values))
    rounded = lax.reduce_precision(factor, 8, 7)
    coarse, fine = rounded.astype(jnp.bfloat16), (factor - rounded).astype(jnp.bfloat16)
    tagged = jnp.concatenate([masked, coarse, fine], axis=1)
    mine = gather_line(masked, 2, 6, half_of)
    middle = jnp.concatenate(mine[1:3], axis=0)
    end = jnp.concatenate(mine[3:], axis=0)
    rows = [masked, middle, end] + [lax.ppermute(part, "samp", samp_perm(1)) for part in (masked, middle, end)]
    pieces = gather_line(tagged, BLOCKS, 3 * BLOCKS, lambda block, part: jnp.split(block, 2)[part])[1:]
    near_cols, far_cols = [masked] + pieces[:2], pieces[2:]
    which = ((lax.axis_index("samp") % BLOCKS) ^ lax.axis_index("site")).astype(jnp.int32).reshape(1)

    def pairs(bit, chunks, cols, flops, extra=()):
        lanes = {"near": 2 * NEAR_BLOCKS * height, "far": 2 * height}
        width = sum(col.shape[0] for col in cols)
        return kernel_call(
            functools.partial(pair_body, bit, chunks),
            [jax.ShapeDtypeStruct((4, height, sum(lanes[chunk] for chunk in chunks)), f32)] * 3 + list(extra),
            scratch=[pltpu.VMEM((BLOCKS, height, sites), jnp.bfloat16)] + [pltpu.VMEM((width, sites), jnp.bfloat16)] * 3,
            smem=1,
            limit=PAIR_VMEM_LIMIT,
            cost=pl.CostEstimate(flops=flops, bytes_accessed=100000, transcendentals=0),
        )(which, *rows, *cols)

    send_near = pairs(1, ("near",), near_cols, 1000000)
    came_near = [lax.ppermute(send_near[r], "site", site_perm(ROUTES[r][0])) for r in range(3)]
    far_cols[0], _ = lax.optimization_barrier((far_cols[0], send_near))
    send_far = pairs(1, ("far",), far_cols, 10000000000)
    came_far = [lax.ppermute(send_far[r], "site", site_perm(ROUTES[r][0])) for r in range(3)]
    far_kept, came_near, _ = lax.optimization_barrier((far_cols[1], came_near, send_far))
    gathered_shape = jax.ShapeDtypeStruct(((DEPTHS - 1) * height, columns), f32)
    *keep, gathered = pairs(0, ("near", "far"), near_cols + [far_cols[0], far_kept], 10000000000, [gathered_shape])
    keep, came_far = lax.optimization_barrier((keep, came_far))
    folded = [fold(keep[r], came_near[r], came_far[r]) for r in range(3)]
    came2 = [lax.ppermute(folded[r][0], "site", site_perm(ROUTES[r][1])) for r in range(3)]
    send = [folded[r][1] + came2[r][1:] for r in range(3)]
    came3 = [lax.ppermute(send[r], "site", site_perm(ROUTES[r][2])) for r in range(3)]
    terms = [t for r in range(3) for t in (folded[r][2], came2[r], came3[r])]
    part = kernel_call(band_body, jax.ShapeDtypeStruct((height, columns), f32))(*terms, gathered, factor)
    part = tree_sum(spread(part, "samp", [1]))
    packed = columns // 2 + PANEL
    message = kernel_call(gram_body, jax.ShapeDtypeStruct((packed + height, columns), f32))(*spread(part, "samp", [2, 4, 6]))
    is_gram = lax.broadcasted_iota(jnp.int32, message.shape, 0) < packed
    apart = which[0]
    came = spread(message, "site", [2, 4, 6])
    turn = apart >> 1
    picked = jnp.where(turn < 2, jnp.where(turn == 0, came[0], came[1]), jnp.where(turn == 2, came[2], came[3]))
    message = jnp.where(is_gram, tree_sum(came), picked)
    came = spread(message, "site", [1])
    message = jnp.where(is_gram, tree_sum(came), jnp.where((apart & 1) == 0, came[0], came[1]))
    gram, own_image = message[:packed], message[packed:]
    gram = tree_sum(spread(gram, "samp", [BLOCKS]))
    grams = spread(gram, "samp", [3 * BLOCKS])
    scale = 1.0 / (height * DEPTHS * BLOCKS)
    basis, triangle = kernel_call(
        functools.partial(factor_body, scale),
        [jax.ShapeDtypeStruct((height, columns), f32), jax.ShapeDtypeStruct((columns, columns), f32)],
        scratch=[pltpu.VMEM((columns, 2 * columns), f32)],
    )(*grams, own_image)
    return (basis, triangle)


def solution(mesh):
    return jax.shard_map(
        local,
        mesh=mesh,
        in_specs=(P("samp", "site"), P("samp", "site"), P("samp", None)),
        out_specs=(P("samp", None), P()),
        check_vma=False,
    )
```

```python
import functools

import jax
import jax.numpy as jnp
from jax import lax
from jax.experimental import pallas as pl
from jax.experimental.pallas import tpu as pltpu
from jax.sharding import PartitionSpec as P

DEPTHS = 4
BLOCKS = 8
SITE_PARTS = 8
PANEL = 8
ROUTES = ((2, 6, 1), (6, 1, 2), (1, 2, 6))
VMEM_LIMIT = 12 * 1024 * 1024
PAIR_VMEM_LIMIT = 22 * 1024 * 1024


def correlate(counts, sum_row, sum_col, sq_row, sq_col, cross):
    numer = counts * cross - sum_row * sum_col
    var_row = counts * sq_row - sum_row * sum_row + counts + 1.0
    var_col = counts * sq_col - sum_col * sum_col + counts + 1.0
    return numer / jnp.sqrt(var_row * var_col)


def square_of(masked):
    return masked * masked


def held_of(masked):
    return jnp.minimum(masked * 16, 1)


def contract(lhs, rhs):
    return lax.dot_general(lhs, rhs, (((1,), (1,)), ((), ())), preferred_element_type=jnp.float32)


def tree_sum(parts):
    parts = list(parts)
    while len(parts) > 1:
        parts = [parts[i] + parts[i + 1] for i in range(0, len(parts), 2)]
    return parts[0]


def kernel_call(body, out_shape, scratch=(), smem=0, cost=None, limit=VMEM_LIMIT):
    params = pltpu.CompilerParams(vmem_limit_bytes=limit)

    def call(*args):
        in_specs = [pl.BlockSpec(memory_space=pltpu.SMEM)] * smem
        in_specs += [pl.BlockSpec(memory_space=pltpu.VMEM)] * (len(args) - smem)
        return pl.pallas_call(
            body,
            out_shape=out_shape,
            in_specs=in_specs,
            out_specs=jax.tree.map(lambda _: pl.BlockSpec(memory_space=pltpu.VMEM), out_shape),
            scratch_shapes=list(scratch),
            compiler_params=params,
            cost_estimate=cost,
        )(*args)

    return call


ROW_PIECES = ((0,), (2, 6), (4,), (1,), (3, 7), (5,))
NEAR_BLOCKS = 3


def route_offsets(route, bit):
    first, second, third = ROUTES[route]
    return [(bit * first) ^ (two * second) ^ (three * third) for two in range(2) for three in range(2)]


def pair_body(bit, chunks, which, *refs):
    n_rows = len(ROW_PIECES)
    rows = refs[:n_rows]
    whole = len(chunks) == 2
    cols, outs = refs[n_rows : -7 - whole], refs[-7 - whole : -4 - whole]
    stack, masked, square, held = refs[-4:]
    height = stack.shape[1]
    sites = masked.shape[1]
    for ref, slots in zip(rows, ROW_PIECES):
        for at, slot in enumerate(slots):
            stack[slot] = ref[at * height : (at + 1) * height]
    begin = 0
    for ref in cols:
        block = ref[:, :sites]
        span = slice(begin, begin + block.shape[0])
        masked[span] = block
        square[span] = square_of(block)
        held[span] = held_of(block)
        if whole and begin > 0:
            columns = (ref.shape[1] - sites) // 2
            gathered = ref[:, sites : sites + columns].astype(jnp.float32) + ref[:, sites + columns :].astype(jnp.float32)
            refs[-5][begin - height : begin - height + block.shape[0]] = gathered
        begin += block.shape[0]
    blocks = [
        jnp.concatenate([stack[which[0] ^ k] for k in route_offsets(route, bit)], axis=0) for route in range(3)
    ]
    by_held = contract(jnp.concatenate([held_of(blocks[0]), blocks[0], square_of(blocks[1])], axis=0), held[...])
    by_masked = contract(jnp.concatenate([held_of(blocks[1]), blocks[2]], axis=0), masked[...])
    by_square = contract(held_of(blocks[2]), square[...])
    count = 4 * height
    sums = (
        (by_held[:count], by_held[count : 2 * count]),
        (by_masked[:count], by_held[2 * count :]),
        (by_square, by_masked[count:]),
    )
    for out, (first, second) in zip(outs, sums):
        at, parts = 0, []
        for chunk in chunks:
            if chunk == "near":
                at = 2 * height
                parts += [first[:, :at], second[:, :at]]
            parts.append(jnp.concatenate([first[:, at : at + height], second[:, at : at + height]], axis=1))
            at += height
        joined = parts[0] if len(parts) == 1 else jnp.concatenate(parts, axis=1)
        for k in range(4):
            out[k] = joined[k * height : (k + 1) * height]


def fold_body(keep, near, far, send, later, last):
    edge = near.shape[2]
    for out, begin in ((send, 2), (later, 1), (last, 0)):
        span = slice(begin, begin + out.shape[0])
        out[:, :, :edge] = keep[span, :, :edge] + near[span]
        out[:, :, edge:] = keep[span, :, edge:] + far[span]


def fold(keep, near, far):
    shapes = [jax.ShapeDtypeStruct((count,) + keep.shape[1:], jnp.float32) for count in (2, 1, 1)]
    return kernel_call(fold_body, shapes)(keep, near, far)


def band_body(*refs):
    whole, gathered, own, out = refs[:9], refs[9], refs[10], refs[11]
    height = own.shape[0]
    edge = 2 * NEAR_BLOCKS * height
    totals = []
    for r in range(3):
        rest = (whole[3 * r][0] + whole[3 * r + 1][0]) + whole[3 * r + 2][0]
        front, back = rest[:, :edge], rest[:, edge:]
        for m in range(2):
            third = slice((4 + m) * height, (5 + m) * height)
            totals.append(
                jnp.concatenate(
                    [
                        front[:, 2 * m * height : 2 * (m + 1) * height],
                        jnp.concatenate([front[:, third], back[:, m * height : (m + 1) * height]], axis=1),
                    ],
                    axis=1,
                )
            )
    band = correlate(*totals)
    factor = jnp.concatenate([own[...], gathered[...]], axis=0)
    out[...] = jnp.dot(band, factor, precision=lax.Precision.HIGHEST, preferred_element_type=jnp.float32)


def gram_body(*refs):
    out = refs[-1]
    image = line_sum([r[...] for r in refs[:-1]])
    gram = lax.dot_general(
        image, image, (((0,), (0,)), ((), ())), precision=lax.Precision.HIGHEST, preferred_element_type=jnp.float32
    )
    packed, diagonal = pack_gram(gram)
    half = packed.shape[0]
    out[:half] = packed
    out[half : half + PANEL] = diagonal
    out[half + PANEL :] = image


def pack_gram(gram):
    half = gram.shape[0] // 2
    rows = lax.broadcasted_iota(jnp.int32, (half, half), 0)
    cols = lax.broadcasted_iota(jnp.int32, (half, half), 1)
    first = jnp.where(cols < rows, gram[half:, half:], gram[:half, :half])
    lane = lax.broadcasted_iota(jnp.int32, (half, 2 * half), 1)
    row = lax.broadcasted_iota(jnp.int32, (half, 2 * half), 0)
    diagonal = jnp.sum(jnp.where(lane == row + half, gram[half:], 0.0), axis=0, keepdims=True)
    return jnp.concatenate([first, gram[:half, half:]], axis=1), jnp.broadcast_to(diagonal, (PANEL, 2 * half))


def unpack_gram(packed, diagonal):
    half = packed.shape[0]
    lane = lax.broadcasted_iota(jnp.int32, (half, 2 * half), 1)
    row = lax.broadcasted_iota(jnp.int32, (half, 2 * half), 0) + half
    turned = packed[:, :half].T
    turned = jnp.concatenate([turned, turned], axis=1)
    return packed, jnp.where(lane == row, diagonal, turned)


def factor_body(scale, *refs):
    grams, (image_ref, basis_ref, triangle_ref, work) = refs[:2], refs[2:]
    size = work.shape[0]
    half = size // 2
    total = tree_sum([gram[...] for gram in grams]) * scale
    top, bottom = unpack_gram(total[:half], total[half : half + 1])
    rows = lax.broadcasted_iota(jnp.int32, (size, size), 0)
    cols = lax.broadcasted_iota(jnp.int32, (size, size), 1)
    shape = (PANEL, size)
    lane = lax.broadcasted_iota(jnp.int32, shape, 1)
    line = lax.broadcasted_iota(jnp.int32, shape, 0)
    count = size // PANEL
    per_half = count // 2
    left_tiles = [
        (top if t < per_half else bottom)[(t % per_half) * PANEL : (t % per_half + 1) * PANEL] for t in range(count)
    ]
    right_tiles = [jnp.where(lane == line + t * PANEL, 1.0, 0.0) for t in range(count)]

    def spread_row(tile, i):
        return jnp.broadcast_to(tile[i : i + 1], shape)

    def spread_lane(row, at):
        return jnp.broadcast_to(row[:, at : at + 1], shape)

    def gather_rows(lines):
        tile = lines[0]
        for i in range(1, PANEL):
            tile = jnp.where(line == i, lines[i], tile)
        return tile

    left = [spread_row(left_tiles[0], i) for i in range(PANEL)]
    right = [spread_row(right_tiles[0], i) for i in range(PANEL)]
    pairs = [(i, j) for i in range(PANEL) for j in range(i, PANEL)]
    pivot = {(i, j): spread_lane(left[i], j) for i, j in pairs}
    for p in range(count):
        start, following = p * PANEL, (p + 1) * PANEL
        if p + 1 < count:
            next_left = [spread_row(left_tiles[p + 1], i) for i in range(PANEL)]
            next_right = [spread_row(right_tiles[p + 1], i) for i in range(PANEL)]
            next_pivot = {(i, j): spread_lane(next_left[i], following + j) for i, j in pairs}
        for k in range(PANEL):
            inverse = lax.rsqrt(pivot[k, k])
            left[k] = left[k] * inverse
            right[k] = right[k] * inverse
            upper = {j: pivot[k, j] * inverse for j in range(k + 1, PANEL)}
            for i in range(k + 1, PANEL):
                left[i] = left[i] - upper[i] * left[k]
                right[i] = right[i] - upper[i] * right[k]
                for j in range(i, PANEL):
                    pivot[i, j] = pivot[i, j] - upper[i] * upper[j]
            if p + 1 < count:
                factors = [spread_lane(left[k], following + i) for i in range(PANEL)]
                for i in range(PANEL):
                    next_left[i] = next_left[i] - factors[i] * left[k]
                    next_right[i] = next_right[i] - factors[i] * right[k]
                for i, j in pairs:
                    next_pivot[i, j] = next_pivot[i, j] - factors[i] * factors[j]
        left_panel, right_panel = gather_rows(left), gather_rows(right)
        work[start:following, :size] = left_panel
        work[start:following, size:] = right_panel
        if p + 2 < count:
            update = lax.dot_general(
                left_panel, jnp.concatenate([left_panel, right_panel], axis=1), (((0,), (0,)), ((), ())),
                precision=lax.Precision.HIGHEST, preferred_element_type=jnp.float32,
            )
            for t in range(p + 2, count):
                span = slice(t * PANEL, (t + 1) * PANEL)
                left_tiles[t] = left_tiles[t] - update[span, :size]
                right_tiles[t] = right_tiles[t] - update[span, size:]
        if p + 1 < count:
            left, right, pivot = next_left, next_right, next_pivot
    upper = jnp.where(cols >= rows, work[:, :size], 0.0)
    triangle_ref[...] = upper.T
    basis_ref[...] = lax.dot_general(
        image_ref[...], work[:, size:], (((1,), (1,)), ((), ())),
        precision=lax.Precision.HIGHEST, preferred_element_type=jnp.float32,
    )


def samp_perm(shift):
    return [(i, i ^ shift) for i in range(DEPTHS * BLOCKS)]


def site_perm(shift):
    return [(i, i ^ shift) for i in range(SITE_PARTS)]


def half_body(part, whole, out):
    count = out.shape[0]
    out[...] = whole[part * count : (part + 1) * count]


def half_of(block, part):
    shape = jax.ShapeDtypeStruct((block.shape[0] // 2, block.shape[1]), block.dtype)
    return kernel_call(functools.partial(half_body, part), shape)(block)


def gather_line(block, near, other, cut):
    one = lax.ppermute(block, "samp", samp_perm(near))
    three = lax.ppermute(block, "samp", samp_perm(other))
    top = lax.ppermute(cut(one, 0), "samp", samp_perm(other))
    bottom = lax.ppermute(cut(three, 1), "samp", samp_perm(near))
    return [block, one, three, top, bottom]


def spread(part, axis, shifts):
    perm = samp_perm if axis == "samp" else site_perm
    return [part] + [lax.ppermute(part, axis, perm(k)) for k in shifts]


def line_sum(parts):
    own, two, one, three = parts
    return (own + one) + (two + three)


def local(values, mask, factor):
    height, sites = values.shape
    columns = factor.shape[1]
    f32 = jnp.float32
    masked = jnp.where(mask == 1, values, jnp.zeros_like(values))
    rounded = lax.reduce_precision(factor, 8, 7)
    coarse, fine = rounded.astype(jnp.bfloat16), (factor - rounded).astype(jnp.bfloat16)
    tagged = jnp.concatenate([masked, coarse, fine], axis=1)
    mine = gather_line(masked, 2, 6, half_of)
    middle = jnp.concatenate(mine[1:3], axis=0)
    end = jnp.concatenate(mine[3:], axis=0)
    rows = [masked, middle, end] + [lax.ppermute(part, "samp", samp_perm(1)) for part in (masked, middle, end)]
    pieces = gather_line(tagged, BLOCKS, 3 * BLOCKS, lambda block, part: jnp.split(block, 2)[part])[1:]
    near_cols, far_cols = [masked] + pieces[:2], pieces[2:]
    which = ((lax.axis_index("samp") % BLOCKS) ^ lax.axis_index("site")).astype(jnp.int32).reshape(1)

    def pairs(bit, chunks, cols, flops, extra=()):
        lanes = {"near": 2 * NEAR_BLOCKS * height, "far": 2 * height}
        width = sum(col.shape[0] for col in cols)
        return kernel_call(
            functools.partial(pair_body, bit, chunks),
            [jax.ShapeDtypeStruct((4, height, sum(lanes[chunk] for chunk in chunks)), f32)] * 3 + list(extra),
            scratch=[pltpu.VMEM((BLOCKS, height, sites), jnp.bfloat16)] + [pltpu.VMEM((width, sites), jnp.bfloat16)] * 3,
            smem=1,
            limit=PAIR_VMEM_LIMIT,
            cost=pl.CostEstimate(flops=flops, bytes_accessed=100000, transcendentals=0),
        )(which, *rows, *cols)

    send_near = pairs(1, ("near",), near_cols, 1000000)
    came_near = [lax.ppermute(send_near[r], "site", site_perm(ROUTES[r][0])) for r in range(3)]
    far_cols[0], _ = lax.optimization_barrier((far_cols[0], send_near))
    send_far = pairs(1, ("far",), far_cols, 10000000000)
    came_far = [lax.ppermute(send_far[r], "site", site_perm(ROUTES[r][0])) for r in range(3)]
    far_kept, came_near, _ = lax.optimization_barrier((far_cols[1], came_near, send_far))
    gathered_shape = jax.ShapeDtypeStruct(((DEPTHS - 1) * height, columns), f32)
    *keep, gathered = pairs(0, ("near", "far"), near_cols + [far_cols[0], far_kept], 10000000000, [gathered_shape])
    keep, came_far = lax.optimization_barrier((keep, came_far))
    folded = [fold(keep[r], came_near[r], came_far[r]) for r in range(3)]
    came2 = [lax.ppermute(folded[r][0], "site", site_perm(ROUTES[r][1])) for r in range(3)]
    send = [folded[r][1] + came2[r][1:] for r in range(3)]
    came3 = [lax.ppermute(send[r], "site", site_perm(ROUTES[r][2])) for r in range(3)]
    terms = [t for r in range(3) for t in (folded[r][2], came2[r], came3[r])]
    part = kernel_call(band_body, jax.ShapeDtypeStruct((height, columns), f32))(*terms, gathered, factor)
    part = tree_sum(spread(part, "samp", [1]))
    packed = columns // 2 + PANEL
    message = kernel_call(gram_body, jax.ShapeDtypeStruct((packed + height, columns), f32))(*spread(part, "samp", [4, 2, 6]))
    is_gram = lax.broadcasted_iota(jnp.int32, message.shape, 0) < packed
    apart = which[0]
    came = spread(message, "site", [4, 2, 6])
    turn = apart >> 1
    picked = jnp.where(turn < 2, jnp.where(turn == 0, came[0], came[2]), jnp.where(turn == 2, came[1], came[3]))
    message = jnp.where(is_gram, line_sum(came), picked)
    came = spread(message, "site", [1])
    message = jnp.where(is_gram, tree_sum(came), jnp.where((apart & 1) == 0, came[0], came[1]))
    gram, own_image = message[:packed], message[packed:]
    gram = tree_sum(spread(gram, "samp", [BLOCKS]))
    grams = spread(gram, "samp", [3 * BLOCKS])
    scale = 1.0 / (height * DEPTHS * BLOCKS)
    basis, triangle = kernel_call(
        functools.partial(factor_body, scale),
        [jax.ShapeDtypeStruct((height, columns), f32), jax.ShapeDtypeStruct((columns, columns), f32)],
        scratch=[pltpu.VMEM((columns, 2 * columns), f32)],
    )(*grams, own_image)
    return (basis, triangle)


def solution(mesh):
    return jax.shard_map(
        local,
        mesh=mesh,
        in_specs=(P("samp", "site"), P("samp", "site"), P("samp", None)),
        out_specs=(P("samp", None), P()),
        check_vma=False,
    )
```

```python
import functools

import jax
import jax.numpy as jnp
from jax import lax
from jax.experimental import pallas as pl
from jax.experimental.pallas import tpu as pltpu
from jax.sharding import PartitionSpec as P

DEPTHS = 4
BLOCKS = 8
SITE_PARTS = 8
PANEL = 8
ROUTES = ((2, 6, 1), (6, 1, 2), (1, 2, 6))
VMEM_LIMIT = 12 * 1024 * 1024
PAIR_VMEM_LIMIT = 22 * 1024 * 1024


def correlate(counts, sum_row, sum_col, sq_row, sq_col, cross):
    numer = counts * cross - sum_row * sum_col
    var_row = counts * sq_row - sum_row * sum_row + counts + 1.0
    var_col = counts * sq_col - sum_col * sum_col + counts + 1.0
    return numer / jnp.sqrt(var_row * var_col)


def square_of(masked):
    return masked * masked


def held_of(masked):
    return jnp.minimum(masked * 16, 1)


def contract(lhs, rhs):
    return lax.dot_general(lhs, rhs, (((1,), (1,)), ((), ())), preferred_element_type=jnp.float32)


def tree_sum(parts):
    parts = list(parts)
    while len(parts) > 1:
        parts = [parts[i] + parts[i + 1] for i in range(0, len(parts), 2)]
    return parts[0]


def kernel_call(body, out_shape, scratch=(), smem=0, cost=None, limit=VMEM_LIMIT):
    params = pltpu.CompilerParams(vmem_limit_bytes=limit)

    def call(*args):
        in_specs = [pl.BlockSpec(memory_space=pltpu.SMEM)] * smem
        in_specs += [pl.BlockSpec(memory_space=pltpu.VMEM)] * (len(args) - smem)
        return pl.pallas_call(
            body,
            out_shape=out_shape,
            in_specs=in_specs,
            out_specs=jax.tree.map(lambda _: pl.BlockSpec(memory_space=pltpu.VMEM), out_shape),
            scratch_shapes=list(scratch),
            compiler_params=params,
            cost_estimate=cost,
        )(*args)

    return call


ROW_PIECES = ((0,), (2, 6), (4,), (1,), (3, 7), (5,))
NEAR_BLOCKS = 3


def route_offsets(route, bit):
    first, second, third = ROUTES[route]
    return [(bit * first) ^ (two * second) ^ (three * third) for two in range(2) for three in range(2)]


def pair_body(bit, chunks, which, *refs):
    n_rows = len(ROW_PIECES)
    rows = refs[:n_rows]
    whole = len(chunks) == 2
    cols, outs = refs[n_rows : -7 - whole], refs[-7 - whole : -4 - whole]
    stack, masked, square, held = refs[-4:]
    height = stack.shape[1]
    sites = masked.shape[1]
    for ref, slots in zip(rows, ROW_PIECES):
        for at, slot in enumerate(slots):
            stack[slot] = ref[at * height : (at + 1) * height]
    begin = 0
    for ref in cols:
        block = ref[:, :sites]
        span = slice(begin, begin + block.shape[0])
        masked[span] = block
        square[span] = square_of(block)
        held[span] = held_of(block)
        if whole and begin > 0:
            columns = (ref.shape[1] - sites) // 2
            gathered = ref[:, sites : sites + columns].astype(jnp.float32) + ref[:, sites + columns :].astype(jnp.float32)
            refs[-5][begin - height : begin - height + block.shape[0]] = gathered
        begin += block.shape[0]
    blocks = [
        jnp.concatenate([stack[which[0] ^ k] for k in route_offsets(route, bit)], axis=0) for route in range(3)
    ]
    by_held = contract(jnp.concatenate([held_of(blocks[0]), blocks[0], square_of(blocks[1])], axis=0), held[...])
    by_masked = contract(jnp.concatenate([held_of(blocks[1]), blocks[2]], axis=0), masked[...])
    by_square = contract(held_of(blocks[2]), square[...])
    count = 4 * height
    sums = (
        (by_held[:count], by_held[count : 2 * count]),
        (by_masked[:count], by_held[2 * count :]),
        (by_square, by_masked[count:]),
    )
    for out, (first, second) in zip(outs, sums):
        at, parts = 0, []
        for chunk in chunks:
            if chunk == "near":
                at = 2 * height
                parts += [first[:, :at], second[:, :at]]
            parts.append(jnp.concatenate([first[:, at : at + height], second[:, at : at + height]], axis=1))
            at += height
        joined = parts[0] if len(parts) == 1 else jnp.concatenate(parts, axis=1)
        for k in range(4):
            out[k] = joined[k * height : (k + 1) * height]


def fold_body(keep, near, far, send, later, last):
    edge = near.shape[2]
    for out, begin in ((send, 2), (later, 1), (last, 0)):
        span = slice(begin, begin + out.shape[0])
        out[:, :, :edge] = keep[span, :, :edge] + near[span]
        out[:, :, edge:] = keep[span, :, edge:] + far[span]


def fold(keep, near, far):
    shapes = [jax.ShapeDtypeStruct((count,) + keep.shape[1:], jnp.float32) for count in (2, 1, 1)]
    return kernel_call(fold_body, shapes)(keep, near, far)


def band_body(*refs):
    whole, gathered, own, out = refs[:9], refs[9], refs[10], refs[11]
    height = own.shape[0]
    edge = 2 * NEAR_BLOCKS * height
    totals = []
    for r in range(3):
        rest = (whole[3 * r][0] + whole[3 * r + 1][0]) + whole[3 * r + 2][0]
        front, back = rest[:, :edge], rest[:, edge:]
        for m in range(2):
            third = slice((4 + m) * height, (5 + m) * height)
            totals.append(
                jnp.concatenate(
                    [
                        front[:, 2 * m * height : 2 * (m + 1) * height],
                        jnp.concatenate([front[:, third], back[:, m * height : (m + 1) * height]], axis=1),
                    ],
                    axis=1,
                )
            )
    band = correlate(*totals)
    factor = jnp.concatenate([own[...], gathered[...]], axis=0)
    out[...] = jnp.dot(band, factor, precision=lax.Precision.HIGHEST, preferred_element_type=jnp.float32)


def gram_body(*refs):
    out = refs[-1]
    image = line_sum([r[...] for r in refs[:-1]])
    gram = lax.dot_general(
        image, image, (((0,), (0,)), ((), ())), precision=lax.Precision.HIGHEST, preferred_element_type=jnp.float32
    )
    packed, diagonal = pack_gram(gram)
    half = packed.shape[0]
    out[:half] = packed
    out[half : half + PANEL] = diagonal
    out[half + PANEL :] = image


def pack_gram(gram):
    half = gram.shape[0] // 2
    rows = lax.broadcasted_iota(jnp.int32, (half, half), 0)
    cols = lax.broadcasted_iota(jnp.int32, (half, half), 1)
    first = jnp.where(cols < rows, gram[half:, half:], gram[:half, :half])
    lane = lax.broadcasted_iota(jnp.int32, (half, 2 * half), 1)
    row = lax.broadcasted_iota(jnp.int32, (half, 2 * half), 0)
    diagonal = jnp.sum(jnp.where(lane == row + half, gram[half:], 0.0), axis=0, keepdims=True)
    return jnp.concatenate([first, gram[:half, half:]], axis=1), jnp.broadcast_to(diagonal, (PANEL, 2 * half))


def unpack_gram(packed, diagonal):
    half = packed.shape[0]
    lane = lax.broadcasted_iota(jnp.int32, (half, 2 * half), 1)
    row = lax.broadcasted_iota(jnp.int32, (half, 2 * half), 0) + half
    turned = packed[:, :half].T
    turned = jnp.concatenate([turned, turned], axis=1)
    return packed, jnp.where(lane == row, diagonal, turned)


def factor_body(scale, *refs):
    grams, (image_ref, basis_ref, triangle_ref, upper_ref, inverse_ref) = refs[:2], refs[2:]
    size = upper_ref.shape[0]
    half = size // 2
    total = tree_sum([gram[...] for gram in grams]) * scale
    top, bottom = unpack_gram(total[:half], total[half : half + 1])
    shape = (PANEL, size)
    lane = lax.broadcasted_iota(jnp.int32, shape, 1)
    line = lax.broadcasted_iota(jnp.int32, shape, 0)
    count = size // PANEL
    per_half = count // 2
    tiles = [(top if t < per_half else bottom)[(t % per_half) * PANEL : (t % per_half + 1) * PANEL] for t in range(count)]

    def spread_row(tile, i):
        return jnp.broadcast_to(tile[i : i + 1], shape)

    def spread_lane(row, at):
        return jnp.broadcast_to(row[:, at : at + 1], shape)

    rows = [spread_row(tiles[0], i) for i in range(PANEL)]
    for p in range(count):
        start, following = p * PANEL, (p + 1) * PANEL
        in_panel = (lane >= start) & (lane < following)
        pivot = {(i, j): spread_lane(rows[i], start + j) for i in range(PANEL) for j in range(i, PANEL)}
        rows = [jnp.where(in_panel, jnp.where(lane == start + i, 1.0, 0.0), rows[i]) for i in range(PANEL)]
        if p + 1 < count:
            cleared = jnp.where(in_panel, 0.0, tiles[p + 1])
            next_rows = [spread_row(cleared, i) for i in range(PANEL)]
        upper_tile = jnp.zeros(shape, jnp.float32)
        for k in range(PANEL):
            inverse = lax.rsqrt(pivot[k, k])
            rows[k] = rows[k] * inverse
            upper = {j: pivot[k, j] * inverse for j in range(k, PANEL)}
            for i in range(k + 1, PANEL):
                rows[i] = rows[i] - upper[i] * rows[k]
                for j in range(i, PANEL):
                    pivot[i, j] = pivot[i, j] - upper[i] * upper[j]
            if p + 1 < count:
                for i in range(PANEL):
                    next_rows[i] = next_rows[i] - spread_lane(rows[k], following + i) * rows[k]
            upper_line = jnp.where(lane >= following, rows[k], 0.0)
            for j in range(k, PANEL):
                upper_line = jnp.where(lane == start + j, upper[j], upper_line)
            upper_tile = jnp.where(line == k, upper_line, upper_tile)
        panel = rows[0]
        for k in range(1, PANEL):
            panel = jnp.where(line == k, rows[k], panel)
        upper_ref[start:following] = upper_tile
        inverse_ref[start:following] = jnp.where(lane < following, panel, 0.0)
        if p + 2 < count:
            update = lax.dot_general(
                panel, panel, (((0,), (0,)), ((), ())),
                precision=lax.Precision.HIGHEST, preferred_element_type=jnp.float32,
            )
            for t in range(p + 2, count):
                tiles[t] = jnp.where(in_panel, 0.0, tiles[t]) - update[t * PANEL : (t + 1) * PANEL]
        if p + 1 < count:
            rows = next_rows
    triangle_ref[...] = upper_ref[...].T
    basis_ref[...] = lax.dot_general(
        image_ref[...], inverse_ref[...], (((1,), (1,)), ((), ())),
        precision=lax.Precision.HIGHEST, preferred_element_type=jnp.float32,
    )


def samp_perm(shift):
    return [(i, i ^ shift) for i in range(DEPTHS * BLOCKS)]


def site_perm(shift):
    return [(i, i ^ shift) for i in range(SITE_PARTS)]


def half_body(part, whole, out):
    count = out.shape[0]
    out[...] = whole[part * count : (part + 1) * count]


def half_of(block, part):
    shape = jax.ShapeDtypeStruct((block.shape[0] // 2, block.shape[1]), block.dtype)
    return kernel_call(functools.partial(half_body, part), shape)(block)


def gather_line(block, near, other, cut):
    one = lax.ppermute(block, "samp", samp_perm(near))
    three = lax.ppermute(block, "samp", samp_perm(other))
    top = lax.ppermute(cut(one, 0), "samp", samp_perm(other))
    bottom = lax.ppermute(cut(three, 1), "samp", samp_perm(near))
    return [block, one, three, top, bottom]


def spread(part, axis, shifts):
    perm = samp_perm if axis == "samp" else site_perm
    return [part] + [lax.ppermute(part, axis, perm(k)) for k in shifts]


def line_sum(parts):
    own, two, one, three = parts
    return (two + three) + (own + one)


def local(values, mask, factor):
    height, sites = values.shape
    columns = factor.shape[1]
    f32 = jnp.float32
    masked = jnp.where(mask == 1, values, jnp.zeros_like(values))
    rounded = lax.reduce_precision(factor, 8, 7)
    coarse, fine = rounded.astype(jnp.bfloat16), (factor - rounded).astype(jnp.bfloat16)
    tagged = jnp.concatenate([masked, coarse, fine], axis=1)
    mine = gather_line(masked, 2, 6, half_of)
    middle = jnp.concatenate(mine[1:3], axis=0)
    end = jnp.concatenate(mine[3:], axis=0)
    rows = [masked, middle, end] + [lax.ppermute(part, "samp", samp_perm(1)) for part in (masked, middle, end)]
    pieces = gather_line(tagged, BLOCKS, 3 * BLOCKS, lambda block, part: jnp.split(block, 2)[part])[1:]
    near_cols, far_cols = [masked] + pieces[:2], pieces[2:]
    which = ((lax.axis_index("samp") % BLOCKS) ^ lax.axis_index("site")).astype(jnp.int32).reshape(1)

    def pairs(bit, chunks, cols, flops, extra=()):
        lanes = {"near": 2 * NEAR_BLOCKS * height, "far": 2 * height}
        width = sum(col.shape[0] for col in cols)
        return kernel_call(
            functools.partial(pair_body, bit, chunks),
            [jax.ShapeDtypeStruct((4, height, sum(lanes[chunk] for chunk in chunks)), f32)] * 3 + list(extra),
            scratch=[pltpu.VMEM((BLOCKS, height, sites), jnp.bfloat16)] + [pltpu.VMEM((width, sites), jnp.bfloat16)] * 3,
            smem=1,
            limit=PAIR_VMEM_LIMIT,
            cost=pl.CostEstimate(flops=flops, bytes_accessed=100000, transcendentals=0),
        )(which, *rows, *cols)

    send_near = pairs(1, ("near",), near_cols, 1000000)
    came_near = [lax.ppermute(send_near[r], "site", site_perm(ROUTES[r][0])) for r in range(3)]
    far_cols[0], _ = lax.optimization_barrier((far_cols[0], send_near))
    send_far = pairs(1, ("far",), far_cols, 10000000000)
    came_far = [lax.ppermute(send_far[r], "site", site_perm(ROUTES[r][0])) for r in range(3)]
    far_kept, came_near, _ = lax.optimization_barrier((far_cols[1], came_near, send_far))
    gathered_shape = jax.ShapeDtypeStruct(((DEPTHS - 1) * height, columns), f32)
    *keep, gathered = pairs(0, ("near", "far"), near_cols + [far_cols[0], far_kept], 10000000000, [gathered_shape])
    keep, came_far = lax.optimization_barrier((keep, came_far))
    folded = [fold(keep[r], came_near[r], came_far[r]) for r in range(3)]
    came2 = [lax.ppermute(folded[r][0], "site", site_perm(ROUTES[r][1])) for r in range(3)]
    send = [folded[r][1] + came2[r][1:] for r in range(3)]
    came3 = [lax.ppermute(send[r], "site", site_perm(ROUTES[r][2])) for r in range(3)]
    terms = [t for r in range(3) for t in (folded[r][2], came2[r], came3[r])]
    part = kernel_call(band_body, jax.ShapeDtypeStruct((height, columns), f32))(*terms, gathered, factor)
    part = tree_sum(spread(part, "samp", [1]))
    packed = columns // 2 + PANEL
    message = kernel_call(gram_body, jax.ShapeDtypeStruct((packed + height, columns), f32))(*spread(part, "samp", [4, 2, 6]))
    is_gram = lax.broadcasted_iota(jnp.int32, message.shape, 0) < packed
    apart = which[0]
    came = spread(message, "site", [4, 2, 6])
    turn = apart >> 1
    picked = jnp.where(turn < 2, jnp.where(turn == 0, came[0], came[2]), jnp.where(turn == 2, came[1], came[3]))
    message = jnp.where(is_gram, line_sum(came), picked)
    came = spread(message, "site", [1])
    message = jnp.where(is_gram, tree_sum(came), jnp.where((apart & 1) == 0, came[0], came[1]))
    gram, own_image = message[:packed], message[packed:]
    gram = tree_sum(spread(gram, "samp", [BLOCKS]))
    grams = spread(gram, "samp", [3 * BLOCKS])
    scale = 1.0 / (height * DEPTHS * BLOCKS)
    basis, triangle = kernel_call(
        functools.partial(factor_body, scale),
        [jax.ShapeDtypeStruct((height, columns), f32), jax.ShapeDtypeStruct((columns, columns), f32)],
        scratch=[pltpu.VMEM((columns, columns), f32)] * 2,
    )(*grams, own_image)
    return (basis, triangle)


def solution(mesh):
    return jax.shard_map(
        local,
        mesh=mesh,
        in_specs=(P("samp", "site"), P("samp", "site"), P("samp", None)),
        out_specs=(P("samp", None), P()),
        check_vma=False,
    )
```

```python
import functools

import jax
import jax.numpy as jnp
from jax import lax
from jax.experimental import pallas as pl
from jax.experimental.pallas import tpu as pltpu
from jax.sharding import PartitionSpec as P

DEPTHS = 4
BLOCKS = 8
SITE_PARTS = 8
PANEL = 8
ROUTES = ((2, 6, 1), (6, 1, 2), (1, 2, 6))
VMEM_LIMIT = 12 * 1024 * 1024
PAIR_VMEM_LIMIT = 22 * 1024 * 1024


def correlate(counts, sum_row, sum_col, sq_row, sq_col, cross):
    numer = counts * cross - sum_row * sum_col
    var_row = counts * sq_row - sum_row * sum_row + counts + 1.0
    var_col = counts * sq_col - sum_col * sum_col + counts + 1.0
    return numer / jnp.sqrt(var_row * var_col)


def square_of(masked):
    return masked * masked


def held_of(masked):
    return jnp.minimum(masked * 16, 1)


def contract(lhs, rhs):
    return lax.dot_general(lhs, rhs, (((1,), (1,)), ((), ())), preferred_element_type=jnp.float32)


def tree_sum(parts):
    parts = list(parts)
    while len(parts) > 1:
        parts = [parts[i] + parts[i + 1] for i in range(0, len(parts), 2)]
    return parts[0]


def kernel_call(body, out_shape, scratch=(), smem=0, cost=None, limit=VMEM_LIMIT):
    params = pltpu.CompilerParams(vmem_limit_bytes=limit)

    def call(*args):
        in_specs = [pl.BlockSpec(memory_space=pltpu.SMEM)] * smem
        in_specs += [pl.BlockSpec(memory_space=pltpu.VMEM)] * (len(args) - smem)
        return pl.pallas_call(
            body,
            out_shape=out_shape,
            in_specs=in_specs,
            out_specs=jax.tree.map(lambda _: pl.BlockSpec(memory_space=pltpu.VMEM), out_shape),
            scratch_shapes=list(scratch),
            compiler_params=params,
            cost_estimate=cost,
        )(*args)

    return call


ROW_PIECES = ((0,), (2, 6), (4,), (1,), (3, 7), (5,))
NEAR_BLOCKS = 3


def route_offsets(route, bit):
    first, second, third = ROUTES[route]
    return [(bit * first) ^ (two * second) ^ (three * third) for two in range(2) for three in range(2)]


def pair_body(bit, chunks, which, *refs):
    n_rows = len(ROW_PIECES)
    rows = refs[:n_rows]
    whole = len(chunks) == 2
    cols, outs = refs[n_rows : -7 - whole], refs[-7 - whole : -4 - whole]
    stack, masked, square, held = refs[-4:]
    height = stack.shape[1]
    sites = masked.shape[1]
    for ref, slots in zip(rows, ROW_PIECES):
        for at, slot in enumerate(slots):
            stack[slot] = ref[at * height : (at + 1) * height]
    begin = 0
    for ref in cols:
        block = ref[:, :sites]
        span = slice(begin, begin + block.shape[0])
        masked[span] = block
        square[span] = square_of(block)
        held[span] = held_of(block)
        if whole and begin > 0:
            columns = (ref.shape[1] - sites) // 2
            gathered = ref[:, sites : sites + columns].astype(jnp.float32) + ref[:, sites + columns :].astype(jnp.float32)
            refs[-5][begin - height : begin - height + block.shape[0]] = gathered
        begin += block.shape[0]
    blocks = [
        jnp.concatenate([stack[which[0] ^ k] for k in route_offsets(route, bit)], axis=0) for route in range(3)
    ]
    by_held = contract(jnp.concatenate([held_of(blocks[0]), blocks[0], square_of(blocks[1])], axis=0), held[...])
    by_masked = contract(jnp.concatenate([held_of(blocks[1]), blocks[2]], axis=0), masked[...])
    by_square = contract(held_of(blocks[2]), square[...])
    count = 4 * height
    sums = (
        (by_held[:count], by_held[count : 2 * count]),
        (by_masked[:count], by_held[2 * count :]),
        (by_square, by_masked[count:]),
    )
    for out, (first, second) in zip(outs, sums):
        at, parts = 0, []
        for chunk in chunks:
            if chunk == "near":
                at = 2 * height
                parts += [first[:, :at], second[:, :at]]
            parts.append(jnp.concatenate([first[:, at : at + height], second[:, at : at + height]], axis=1))
            at += height
        joined = parts[0] if len(parts) == 1 else jnp.concatenate(parts, axis=1)
        for k in range(4):
            out[k] = joined[k * height : (k + 1) * height]


def fold_body(keep, near, far, send, later, last):
    edge = near.shape[2]
    for out, begin in ((send, 2), (later, 1), (last, 0)):
        span = slice(begin, begin + out.shape[0])
        out[:, :, :edge] = keep[span, :, :edge] + near[span]
        out[:, :, edge:] = keep[span, :, edge:] + far[span]


def fold(keep, near, far):
    shapes = [jax.ShapeDtypeStruct((count,) + keep.shape[1:], jnp.float32) for count in (2, 1, 1)]
    return kernel_call(fold_body, shapes)(keep, near, far)


def band_body(*refs):
    whole, gathered, own, out = refs[:9], refs[9], refs[10], refs[11]
    height = own.shape[0]
    edge = 2 * NEAR_BLOCKS * height
    totals = []
    for r in range(3):
        rest = (whole[3 * r][0] + whole[3 * r + 1][0]) + whole[3 * r + 2][0]
        front, back = rest[:, :edge], rest[:, edge:]
        for m in range(2):
            third = slice((4 + m) * height, (5 + m) * height)
            totals.append(
                jnp.concatenate(
                    [
                        front[:, 2 * m * height : 2 * (m + 1) * height],
                        jnp.concatenate([front[:, third], back[:, m * height : (m + 1) * height]], axis=1),
                    ],
                    axis=1,
                )
            )
    band = correlate(*totals)
    factor = jnp.concatenate([own[...], gathered[...]], axis=0)
    out[...] = jnp.dot(band, factor, precision=lax.Precision.HIGHEST, preferred_element_type=jnp.float32)


def gram_body(*refs):
    out = refs[-1]
    image = line_sum([r[...] for r in refs[:-1]])
    gram = lax.dot_general(
        image, image, (((0,), (0,)), ((), ())), precision=lax.Precision.HIGHEST, preferred_element_type=jnp.float32
    )
    packed, diagonal = pack_gram(gram)
    half = packed.shape[0]
    out[:half] = packed
    out[half : half + PANEL] = diagonal
    out[half + PANEL :] = image


def pack_gram(gram):
    half = gram.shape[0] // 2
    rows = lax.broadcasted_iota(jnp.int32, (half, half), 0)
    cols = lax.broadcasted_iota(jnp.int32, (half, half), 1)
    first = jnp.where(cols < rows, gram[half:, half:], gram[:half, :half])
    lane = lax.broadcasted_iota(jnp.int32, (half, 2 * half), 1)
    row = lax.broadcasted_iota(jnp.int32, (half, 2 * half), 0)
    diagonal = jnp.sum(jnp.where(lane == row + half, gram[half:], 0.0), axis=0, keepdims=True)
    return jnp.concatenate([first, gram[:half, half:]], axis=1), jnp.broadcast_to(diagonal, (PANEL, 2 * half))


def unpack_gram(packed, diagonal):
    half = packed.shape[0]
    lane = lax.broadcasted_iota(jnp.int32, (half, 2 * half), 1)
    row = lax.broadcasted_iota(jnp.int32, (half, 2 * half), 0) + half
    turned = packed[:, :half].T
    turned = jnp.concatenate([turned, turned], axis=1)
    return packed, jnp.where(lane == row, diagonal, turned)


def factor_body(scale, *refs):
    grams, (image_ref, basis_ref, triangle_ref, upper_ref, inverse_ref) = refs[:DEPTHS], refs[DEPTHS:]
    size = upper_ref.shape[0]
    half = size // 2
    total = line_sum([gram[...] for gram in grams]) * scale
    top, bottom = unpack_gram(total[:half], total[half : half + 1])
    shape = (PANEL, size)
    lane = lax.broadcasted_iota(jnp.int32, shape, 1)
    line = lax.broadcasted_iota(jnp.int32, shape, 0)
    count = size // PANEL
    per_half = count // 2
    tiles = [(top if t < per_half else bottom)[(t % per_half) * PANEL : (t % per_half + 1) * PANEL] for t in range(count)]

    def spread_row(tile, i):
        return jnp.broadcast_to(tile[i : i + 1], shape)

    def spread_lane(row, at):
        return jnp.broadcast_to(row[:, at : at + 1], shape)

    rows = [spread_row(tiles[0], i) for i in range(PANEL)]
    for p in range(count):
        start, following = p * PANEL, (p + 1) * PANEL
        in_panel = (lane >= start) & (lane < following)
        pivot = {(i, j): spread_lane(rows[i], start + j) for i in range(PANEL) for j in range(i, PANEL)}
        rows = [jnp.where(in_panel, jnp.where(lane == start + i, 1.0, 0.0), rows[i]) for i in range(PANEL)]
        if p + 1 < count:
            cleared = jnp.where(in_panel, 0.0, tiles[p + 1])
            next_rows = [spread_row(cleared, i) for i in range(PANEL)]
        upper_tile = jnp.zeros(shape, jnp.float32)
        for k in range(PANEL):
            inverse = lax.rsqrt(pivot[k, k])
            rows[k] = rows[k] * inverse
            upper = {j: pivot[k, j] * inverse for j in range(k, PANEL)}
            for i in range(k + 1, PANEL):
                rows[i] = rows[i] - upper[i] * rows[k]
                for j in range(i, PANEL):
                    pivot[i, j] = pivot[i, j] - upper[i] * upper[j]
            if p + 1 < count:
                for i in range(PANEL):
                    next_rows[i] = next_rows[i] - spread_lane(rows[k], following + i) * rows[k]
            upper_line = jnp.where(lane >= following, rows[k], 0.0)
            for j in range(k, PANEL):
                upper_line = jnp.where(lane == start + j, upper[j], upper_line)
            upper_tile = jnp.where(line == k, upper_line, upper_tile)
        panel = rows[0]
        for k in range(1, PANEL):
            panel = jnp.where(line == k, rows[k], panel)
        upper_ref[start:following] = upper_tile
        inverse_ref[start:following] = jnp.where(lane < following, panel, 0.0)
        if p + 2 < count:
            update = lax.dot_general(
                panel, panel, (((0,), (0,)), ((), ())),
                precision=lax.Precision.HIGHEST, preferred_element_type=jnp.float32,
            )
            for t in range(p + 2, count):
                tiles[t] = jnp.where(in_panel, 0.0, tiles[t]) - update[t * PANEL : (t + 1) * PANEL]
        if p + 1 < count:
            rows = next_rows
    triangle_ref[...] = upper_ref[...].T
    basis_ref[...] = lax.dot_general(
        image_ref[...], inverse_ref[...], (((1,), (1,)), ((), ())),
        precision=lax.Precision.HIGHEST, preferred_element_type=jnp.float32,
    )


def samp_perm(shift):
    return [(i, i ^ shift) for i in range(DEPTHS * BLOCKS)]


def site_perm(shift):
    return [(i, i ^ shift) for i in range(SITE_PARTS)]


def half_body(part, whole, out):
    count = out.shape[0]
    out[...] = whole[part * count : (part + 1) * count]


def half_of(block, part):
    shape = jax.ShapeDtypeStruct((block.shape[0] // 2, block.shape[1]), block.dtype)
    return kernel_call(functools.partial(half_body, part), shape)(block)


def gather_line(block, near, other, cut):
    one = lax.ppermute(block, "samp", samp_perm(near))
    three = lax.ppermute(block, "samp", samp_perm(other))
    top = lax.ppermute(cut(one, 0), "samp", samp_perm(other))
    bottom = lax.ppermute(cut(three, 1), "samp", samp_perm(near))
    return [block, one, three, top, bottom]


def spread(part, axis, shifts):
    perm = samp_perm if axis == "samp" else site_perm
    return [part] + [lax.ppermute(part, axis, perm(k)) for k in shifts]


def line_sum(parts):
    own, two, one, three = parts
    return (two + three) + (own + one)


def local(values, mask, factor):
    height, sites = values.shape
    columns = factor.shape[1]
    f32 = jnp.float32
    masked = jnp.where(mask == 1, values, jnp.zeros_like(values))
    rounded = lax.reduce_precision(factor, 8, 7)
    coarse, fine = rounded.astype(jnp.bfloat16), (factor - rounded).astype(jnp.bfloat16)
    tagged = jnp.concatenate([masked, coarse, fine], axis=1)
    mine = gather_line(masked, 2, 6, half_of)
    middle = jnp.concatenate(mine[1:3], axis=0)
    end = jnp.concatenate(mine[3:], axis=0)
    rows = [masked, middle, end] + [lax.ppermute(part, "samp", samp_perm(1)) for part in (masked, middle, end)]
    pieces = gather_line(tagged, BLOCKS, 3 * BLOCKS, lambda block, part: jnp.split(block, 2)[part])[1:]
    near_cols, far_cols = [masked] + pieces[:2], pieces[2:]
    which = ((lax.axis_index("samp") % BLOCKS) ^ lax.axis_index("site")).astype(jnp.int32).reshape(1)

    def pairs(bit, chunks, cols, flops, extra=()):
        lanes = {"near": 2 * NEAR_BLOCKS * height, "far": 2 * height}
        width = sum(col.shape[0] for col in cols)
        return kernel_call(
            functools.partial(pair_body, bit, chunks),
            [jax.ShapeDtypeStruct((4, height, sum(lanes[chunk] for chunk in chunks)), f32)] * 3 + list(extra),
            scratch=[pltpu.VMEM((BLOCKS, height, sites), jnp.bfloat16)] + [pltpu.VMEM((width, sites), jnp.bfloat16)] * 3,
            smem=1,
            limit=PAIR_VMEM_LIMIT,
            cost=pl.CostEstimate(flops=flops, bytes_accessed=100000, transcendentals=0),
        )(which, *rows, *cols)

    send_near = pairs(1, ("near",), near_cols, 1000000)
    came_near = [lax.ppermute(send_near[r], "site", site_perm(ROUTES[r][0])) for r in range(3)]
    far_cols[0], _ = lax.optimization_barrier((far_cols[0], send_near))
    send_far = pairs(1, ("far",), far_cols, 10000000000)
    came_far = [lax.ppermute(send_far[r], "site", site_perm(ROUTES[r][0])) for r in range(3)]
    far_kept, came_near, _ = lax.optimization_barrier((far_cols[1], came_near, send_far))
    gathered_shape = jax.ShapeDtypeStruct(((DEPTHS - 1) * height, columns), f32)
    *keep, gathered = pairs(0, ("near", "far"), near_cols + [far_cols[0], far_kept], 10000000000, [gathered_shape])
    keep, came_far = lax.optimization_barrier((keep, came_far))
    folded = [fold(keep[r], came_near[r], came_far[r]) for r in range(3)]
    came2 = [lax.ppermute(folded[r][0], "site", site_perm(ROUTES[r][1])) for r in range(3)]
    send = [folded[r][1] + came2[r][1:] for r in range(3)]
    came3 = [lax.ppermute(send[r], "site", site_perm(ROUTES[r][2])) for r in range(3)]
    terms = [t for r in range(3) for t in (folded[r][2], came2[r], came3[r])]
    part = kernel_call(band_body, jax.ShapeDtypeStruct((height, columns), f32))(*terms, gathered, factor)
    part = tree_sum(spread(part, "samp", [1]))
    packed = columns // 2 + PANEL
    message = kernel_call(gram_body, jax.ShapeDtypeStruct((packed + height, columns), f32))(*spread(part, "samp", [4, 2, 6]))
    is_gram = lax.broadcasted_iota(jnp.int32, message.shape, 0) < packed
    apart = which[0]
    came = spread(message, "site", [4, 2, 6])
    turn = apart >> 1
    picked = jnp.where(turn < 2, jnp.where(turn == 0, came[0], came[2]), jnp.where(turn == 2, came[1], came[3]))
    message = jnp.where(is_gram, line_sum(came), picked)
    came = spread(message, "site", [1])
    message = jnp.where(is_gram, tree_sum(came), jnp.where((apart & 1) == 0, came[0], came[1]))
    gram, own_image = message[:packed], message[packed:]
    grams = spread(gram, "samp", [2 * BLOCKS, BLOCKS, 3 * BLOCKS])
    scale = 1.0 / (height * DEPTHS * BLOCKS)
    basis, triangle = kernel_call(
        functools.partial(factor_body, scale),
        [jax.ShapeDtypeStruct((height, columns), f32), jax.ShapeDtypeStruct((columns, columns), f32)],
        scratch=[pltpu.VMEM((columns, columns), f32)] * 2,
    )(*grams, own_image)
    return (basis, triangle)


def solution(mesh):
    return jax.shard_map(
        local,
        mesh=mesh,
        in_specs=(P("samp", "site"), P("samp", "site"), P("samp", None)),
        out_specs=(P("samp", None), P()),
        check_vma=False,
    )
```

```python
import functools

import jax
import jax.numpy as jnp
from jax import lax
from jax.experimental import pallas as pl
from jax.experimental.pallas import tpu as pltpu
from jax.sharding import PartitionSpec as P

DEPTHS = 4
BLOCKS = 8
SITE_PARTS = 8
PANEL = 8
ROUTES = ((2, 6, 1), (1, 2, 6), (6, 1, 2))
VMEM_LIMIT = 12 * 1024 * 1024
PAIR_VMEM_LIMIT = 22 * 1024 * 1024


def correlate(counts, sum_row, sum_col, sq_row, sq_col, cross):
    numer = counts * cross - sum_row * sum_col
    var_row = counts * sq_row - sum_row * sum_row + counts + 1.0
    var_col = counts * sq_col - sum_col * sum_col + counts + 1.0
    return numer / jnp.sqrt(var_row * var_col)


def square_of(masked):
    return masked * masked


def held_of(masked):
    return jnp.minimum(masked * 16, 1)


def contract(lhs, rhs):
    return lax.dot_general(lhs, rhs, (((1,), (1,)), ((), ())), preferred_element_type=jnp.float32)


def tree_sum(parts):
    parts = list(parts)
    while len(parts) > 1:
        parts = [parts[i] + parts[i + 1] for i in range(0, len(parts), 2)]
    return parts[0]


def kernel_call(body, out_shape, scratch=(), smem=0, cost=None, limit=VMEM_LIMIT):
    params = pltpu.CompilerParams(vmem_limit_bytes=limit)

    def call(*args):
        in_specs = [pl.BlockSpec(memory_space=pltpu.SMEM)] * smem
        in_specs += [pl.BlockSpec(memory_space=pltpu.VMEM)] * (len(args) - smem)
        return pl.pallas_call(
            body,
            out_shape=out_shape,
            in_specs=in_specs,
            out_specs=jax.tree.map(lambda _: pl.BlockSpec(memory_space=pltpu.VMEM), out_shape),
            scratch_shapes=list(scratch),
            compiler_params=params,
            cost_estimate=cost,
        )(*args)

    return call


ROW_PIECES = ((0,), (2, 6), (4,), (1,), (3, 7), (5,))
NEAR_BLOCKS = 3


def route_offsets(route, bit):
    first, second, third = ROUTES[route]
    return [(bit * first) ^ (two * second) ^ (three * third) for two in range(2) for three in range(2)]


def pair_body(bit, chunks, which, *refs):
    n_rows = len(ROW_PIECES)
    rows = refs[:n_rows]
    whole = len(chunks) == 2
    cols, outs = refs[n_rows : -7 - whole], refs[-7 - whole : -4 - whole]
    stack, masked, square, held = refs[-4:]
    height = stack.shape[1]
    sites = masked.shape[1]
    for ref, slots in zip(rows, ROW_PIECES):
        for at, slot in enumerate(slots):
            stack[slot] = ref[at * height : (at + 1) * height]
    begin = 0
    for ref in cols:
        block = ref[:, :sites]
        span = slice(begin, begin + block.shape[0])
        masked[span] = block
        square[span] = square_of(block)
        held[span] = held_of(block)
        if whole and begin > 0:
            columns = (ref.shape[1] - sites) // 2
            gathered = ref[:, sites : sites + columns].astype(jnp.float32) + ref[:, sites + columns :].astype(jnp.float32)
            refs[-5][begin - height : begin - height + block.shape[0]] = gathered
        begin += block.shape[0]
    blocks = [
        jnp.concatenate([stack[which[0] ^ k] for k in route_offsets(route, bit)], axis=0) for route in range(3)
    ]
    by_held = contract(jnp.concatenate([held_of(blocks[0]), blocks[0], square_of(blocks[1])], axis=0), held[...])
    by_masked = contract(jnp.concatenate([held_of(blocks[1]), blocks[2]], axis=0), masked[...])
    by_square = contract(held_of(blocks[2]), square[...])
    count = 4 * height
    sums = (
        (by_held[:count], by_held[count : 2 * count]),
        (by_masked[:count], by_held[2 * count :]),
        (by_square, by_masked[count:]),
    )
    for out, (first, second) in zip(outs, sums):
        at, parts = 0, []
        for chunk in chunks:
            if chunk == "near":
                at = 2 * height
                parts += [first[:, :at], second[:, :at]]
            parts.append(jnp.concatenate([first[:, at : at + height], second[:, at : at + height]], axis=1))
            at += height
        joined = parts[0] if len(parts) == 1 else jnp.concatenate(parts, axis=1)
        for k in range(4):
            out[k] = joined[k * height : (k + 1) * height]


def fold_body(keep, near, far, send, later, last):
    edge = near.shape[2]
    for out, begin in ((send, 2), (later, 1), (last, 0)):
        span = slice(begin, begin + out.shape[0])
        out[:, :, :edge] = keep[span, :, :edge] + near[span]
        out[:, :, edge:] = keep[span, :, edge:] + far[span]


def fold(keep, near, far):
    shapes = [jax.ShapeDtypeStruct((count,) + keep.shape[1:], jnp.float32) for count in (2, 1, 1)]
    return kernel_call(fold_body, shapes)(keep, near, far)


def band_body(*refs):
    whole, gathered, own, out = refs[:9], refs[9], refs[10], refs[11]
    height = own.shape[0]
    edge = 2 * NEAR_BLOCKS * height
    totals = []
    for r in range(3):
        rest = (whole[3 * r][0] + whole[3 * r + 1][0]) + whole[3 * r + 2][0]
        front, back = rest[:, :edge], rest[:, edge:]
        for m in range(2):
            third = slice((4 + m) * height, (5 + m) * height)
            totals.append(
                jnp.concatenate(
                    [
                        front[:, 2 * m * height : 2 * (m + 1) * height],
                        jnp.concatenate([front[:, third], back[:, m * height : (m + 1) * height]], axis=1),
                    ],
                    axis=1,
                )
            )
    band = correlate(*totals)
    factor = jnp.concatenate([own[...], gathered[...]], axis=0)
    out[...] = jnp.dot(band, factor, precision=lax.Precision.HIGHEST, preferred_element_type=jnp.float32)


def gram_body(*refs):
    out = refs[-1]
    image = line_sum([r[...] for r in refs[:-1]])
    gram = lax.dot_general(
        image, image, (((0,), (0,)), ((), ())), precision=lax.Precision.HIGHEST, preferred_element_type=jnp.float32
    )
    packed, diagonal = pack_gram(gram)
    half = packed.shape[0]
    out[:half] = packed
    out[half : half + PANEL] = diagonal
    out[half + PANEL :] = image


def pack_gram(gram):
    half = gram.shape[0] // 2
    rows = lax.broadcasted_iota(jnp.int32, (half, half), 0)
    cols = lax.broadcasted_iota(jnp.int32, (half, half), 1)
    first = jnp.where(cols < rows, gram[half:, half:], gram[:half, :half])
    lane = lax.broadcasted_iota(jnp.int32, (half, 2 * half), 1)
    row = lax.broadcasted_iota(jnp.int32, (half, 2 * half), 0)
    diagonal = jnp.sum(jnp.where(lane == row + half, gram[half:], 0.0), axis=0, keepdims=True)
    return jnp.concatenate([first, gram[:half, half:]], axis=1), jnp.broadcast_to(diagonal, (PANEL, 2 * half))


def unpack_gram(packed, diagonal):
    half = packed.shape[0]
    lane = lax.broadcasted_iota(jnp.int32, (half, 2 * half), 1)
    row = lax.broadcasted_iota(jnp.int32, (half, 2 * half), 0) + half
    turned = packed[:, :half].T
    turned = jnp.concatenate([turned, turned], axis=1)
    return packed, jnp.where(lane == row, diagonal, turned)


def factor_body(scale, *refs):
    grams, (image_ref, basis_ref, triangle_ref, upper_ref, inverse_ref) = refs[:DEPTHS], refs[DEPTHS:]
    size = upper_ref.shape[0]
    half = size // 2
    total = line_sum([gram[...] for gram in grams]) * scale
    top, bottom = unpack_gram(total[:half], total[half : half + 1])
    shape = (PANEL, size)
    lane = lax.broadcasted_iota(jnp.int32, shape, 1)
    line = lax.broadcasted_iota(jnp.int32, shape, 0)
    count = size // PANEL
    per_half = count // 2
    tiles = [(top if t < per_half else bottom)[(t % per_half) * PANEL : (t % per_half + 1) * PANEL] for t in range(count)]

    def spread_row(tile, i):
        return jnp.broadcast_to(tile[i : i + 1], shape)

    def spread_lane(row, at):
        return jnp.broadcast_to(row[:, at : at + 1], shape)

    rows = [spread_row(tiles[0], i) for i in range(PANEL)]
    for p in range(count):
        start, following = p * PANEL, (p + 1) * PANEL
        in_panel = (lane >= start) & (lane < following)
        pivot = {(i, j): spread_lane(rows[i], start + j) for i in range(PANEL) for j in range(i, PANEL)}
        rows = [jnp.where(in_panel, jnp.where(lane == start + i, 1.0, 0.0), rows[i]) for i in range(PANEL)]
        if p + 1 < count:
            cleared = jnp.where(in_panel, 0.0, tiles[p + 1])
            next_rows = [spread_row(cleared, i) for i in range(PANEL)]
        upper_tile = jnp.zeros(shape, jnp.float32)
        for k in range(PANEL):
            inverse = lax.rsqrt(pivot[k, k])
            rows[k] = rows[k] * inverse
            upper = {j: pivot[k, j] * inverse for j in range(k, PANEL)}
            for i in range(k + 1, PANEL):
                rows[i] = rows[i] - upper[i] * rows[k]
                for j in range(i, PANEL):
                    pivot[i, j] = pivot[i, j] - upper[i] * upper[j]
            if p + 1 < count:
                for i in range(PANEL):
                    next_rows[i] = next_rows[i] - spread_lane(rows[k], following + i) * rows[k]
            upper_line = jnp.where(lane >= following, rows[k], 0.0)
            for j in range(k, PANEL):
                upper_line = jnp.where(lane == start + j, upper[j], upper_line)
            upper_tile = jnp.where(line == k, upper_line, upper_tile)
        panel = rows[0]
        for k in range(1, PANEL):
            panel = jnp.where(line == k, rows[k], panel)
        upper_ref[start:following] = upper_tile
        inverse_ref[start:following] = jnp.where(lane < following, panel, 0.0)
        if p + 2 < count:
            update = lax.dot_general(
                panel, panel, (((0,), (0,)), ((), ())),
                precision=lax.Precision.HIGHEST, preferred_element_type=jnp.float32,
            )
            for t in range(p + 2, count):
                tiles[t] = jnp.where(in_panel, 0.0, tiles[t]) - update[t * PANEL : (t + 1) * PANEL]
        if p + 1 < count:
            rows = next_rows
    triangle_ref[...] = upper_ref[...].T
    basis_ref[...] = lax.dot_general(
        image_ref[...], inverse_ref[...], (((1,), (1,)), ((), ())),
        precision=lax.Precision.HIGHEST, preferred_element_type=jnp.float32,
    )


def samp_perm(shift):
    return [(i, i ^ shift) for i in range(DEPTHS * BLOCKS)]


def site_perm(shift):
    return [(i, i ^ shift) for i in range(SITE_PARTS)]


def half_body(part, whole, out):
    count = out.shape[0]
    out[...] = whole[part * count : (part + 1) * count]


def half_of(block, part):
    shape = jax.ShapeDtypeStruct((block.shape[0] // 2, block.shape[1]), block.dtype)
    return kernel_call(functools.partial(half_body, part), shape)(block)


def gather_line(block, near, other, cut):
    one = lax.ppermute(block, "samp", samp_perm(near))
    three = lax.ppermute(block, "samp", samp_perm(other))
    top = lax.ppermute(cut(one, 0), "samp", samp_perm(other))
    bottom = lax.ppermute(cut(three, 1), "samp", samp_perm(near))
    return [block, one, three, top, bottom]


def spread(part, axis, shifts):
    perm = samp_perm if axis == "samp" else site_perm
    return [part] + [lax.ppermute(part, axis, perm(k)) for k in shifts]


def line_sum(parts):
    own, two, one, three = parts
    return (two + three) + (own + one)


def local(values, mask, factor):
    height, sites = values.shape
    columns = factor.shape[1]
    f32 = jnp.float32
    masked = jnp.where(mask == 1, values, jnp.zeros_like(values))
    rounded = lax.reduce_precision(factor, 8, 7)
    coarse, fine = rounded.astype(jnp.bfloat16), (factor - rounded).astype(jnp.bfloat16)
    tagged = jnp.concatenate([masked, coarse, fine], axis=1)
    mine = gather_line(masked, 2, 6, half_of)
    middle = jnp.concatenate(mine[1:3], axis=0)
    end = jnp.concatenate(mine[3:], axis=0)
    rows = [masked, middle, end] + [lax.ppermute(part, "samp", samp_perm(1)) for part in (masked, middle, end)]
    pieces = gather_line(tagged, BLOCKS, 3 * BLOCKS, lambda block, part: jnp.split(block, 2)[part])[1:]
    near_cols, far_cols = [masked] + pieces[:2], pieces[2:]
    which = ((lax.axis_index("samp") % BLOCKS) ^ lax.axis_index("site")).astype(jnp.int32).reshape(1)

    def pairs(bit, chunks, cols, flops, extra=()):
        lanes = {"near": 2 * NEAR_BLOCKS * height, "far": 2 * height}
        width = sum(col.shape[0] for col in cols)
        return kernel_call(
            functools.partial(pair_body, bit, chunks),
            [jax.ShapeDtypeStruct((4, height, sum(lanes[chunk] for chunk in chunks)), f32)] * 3 + list(extra),
            scratch=[pltpu.VMEM((BLOCKS, height, sites), jnp.bfloat16)] + [pltpu.VMEM((width, sites), jnp.bfloat16)] * 3,
            smem=1,
            limit=PAIR_VMEM_LIMIT,
            cost=pl.CostEstimate(flops=flops, bytes_accessed=100000, transcendentals=0),
        )(which, *rows, *cols)

    send_near = pairs(1, ("near",), near_cols, 1000000)
    came_near = [lax.ppermute(send_near[r], "site", site_perm(ROUTES[r][0])) for r in range(3)]
    far_cols[0], _ = lax.optimization_barrier((far_cols[0], send_near))
    send_far = pairs(1, ("far",), far_cols, 10000000000)
    came_far = [lax.ppermute(send_far[r], "site", site_perm(ROUTES[r][0])) for r in range(3)]
    far_kept, came_near, _ = lax.optimization_barrier((far_cols[1], came_near, send_far))
    gathered_shape = jax.ShapeDtypeStruct(((DEPTHS - 1) * height, columns), f32)
    *keep, gathered = pairs(0, ("near", "far"), near_cols + [far_cols[0], far_kept], 10000000000, [gathered_shape])
    keep, came_far = lax.optimization_barrier((keep, came_far))
    folded = [fold(keep[r], came_near[r], came_far[r]) for r in range(3)]
    came2 = [lax.ppermute(folded[r][0], "site", site_perm(ROUTES[r][1])) for r in range(3)]
    send = [folded[r][1] + came2[r][1:] for r in range(3)]
    came3 = [lax.ppermute(send[r], "site", site_perm(ROUTES[r][2])) for r in range(3)]
    terms = [t for r in range(3) for t in (folded[r][2], came2[r], came3[r])]
    part = kernel_call(band_body, jax.ShapeDtypeStruct((height, columns), f32))(*terms, gathered, factor)
    part = tree_sum(spread(part, "samp", [1]))
    packed = columns // 2 + PANEL
    message = kernel_call(gram_body, jax.ShapeDtypeStruct((packed + height, columns), f32))(*spread(part, "samp", [4, 2, 6]))
    is_gram = lax.broadcasted_iota(jnp.int32, message.shape, 0) < packed
    apart = which[0]
    came = spread(message, "site", [4, 2, 6])
    turn = apart >> 1
    picked = jnp.where(turn < 2, jnp.where(turn == 0, came[0], came[2]), jnp.where(turn == 2, came[1], came[3]))
    message = jnp.where(is_gram, line_sum(came), picked)
    came = spread(message, "site", [1])
    message = jnp.where(is_gram, tree_sum(came), jnp.where((apart & 1) == 0, came[0], came[1]))
    gram, own_image = message[:packed], message[packed:]
    grams = spread(gram, "samp", [2 * BLOCKS, BLOCKS, 3 * BLOCKS])
    scale = 1.0 / (height * DEPTHS * BLOCKS)
    basis, triangle = kernel_call(
        functools.partial(factor_body, scale),
        [jax.ShapeDtypeStruct((height, columns), f32), jax.ShapeDtypeStruct((columns, columns), f32)],
        scratch=[pltpu.VMEM((columns, columns), f32)] * 2,
    )(*grams, own_image)
    return (basis, triangle)


def solution(mesh):
    return jax.shard_map(
        local,
        mesh=mesh,
        in_specs=(P("samp", "site"), P("samp", "site"), P("samp", None)),
        out_specs=(P("samp", None), P()),
        check_vma=False,
    )
```

```python
import functools

import jax
import jax.numpy as jnp
from jax import lax
from jax.experimental import pallas as pl
from jax.experimental.pallas import tpu as pltpu
from jax.sharding import PartitionSpec as P

DEPTHS = 4
BLOCKS = 8
SITE_PARTS = 8
PANEL = 8
ROUTES = ((2, 6, 1), (6, 1, 2), (1, 2, 6))
VMEM_LIMIT = 12 * 1024 * 1024
PAIR_VMEM_LIMIT = 22 * 1024 * 1024


def correlate(counts, sum_row, sum_col, sq_row, sq_col, cross):
    numer = counts * cross - sum_row * sum_col
    var_row = counts * sq_row - sum_row * sum_row + counts + 1.0
    var_col = counts * sq_col - sum_col * sum_col + counts + 1.0
    return numer / jnp.sqrt(var_row * var_col)


def square_of(masked):
    return masked * masked


def held_of(masked):
    return jnp.minimum(masked * 16, 1)


def contract(lhs, rhs):
    return lax.dot_general(lhs, rhs, (((1,), (1,)), ((), ())), preferred_element_type=jnp.float32)


def tree_sum(parts):
    parts = list(parts)
    while len(parts) > 1:
        parts = [parts[i] + parts[i + 1] for i in range(0, len(parts), 2)]
    return parts[0]


def kernel_call(body, out_shape, scratch=(), smem=0, cost=None, limit=VMEM_LIMIT):
    params = pltpu.CompilerParams(vmem_limit_bytes=limit)

    def call(*args):
        in_specs = [pl.BlockSpec(memory_space=pltpu.SMEM)] * smem
        in_specs += [pl.BlockSpec(memory_space=pltpu.VMEM)] * (len(args) - smem)
        return pl.pallas_call(
            body,
            out_shape=out_shape,
            in_specs=in_specs,
            out_specs=jax.tree.map(lambda _: pl.BlockSpec(memory_space=pltpu.VMEM), out_shape),
            scratch_shapes=list(scratch),
            compiler_params=params,
            cost_estimate=cost,
        )(*args)

    return call


ROW_PIECES = ((0,), (2, 6), (4,), (1,), (3, 7), (5,))
NEAR_BLOCKS = 3


def route_offsets(route, bit):
    first, second, third = ROUTES[route]
    return [(bit * first) ^ (two * second) ^ (three * third) for two in range(2) for three in range(2)]


def pair_body(bit, chunks, which, *refs):
    n_rows = len(ROW_PIECES)
    rows = refs[:n_rows]
    whole = len(chunks) == 2
    cols, outs = refs[n_rows : -7 - whole], refs[-7 - whole : -4 - whole]
    stack, masked, square, held = refs[-4:]
    height = stack.shape[1]
    sites = masked.shape[1]
    for ref, slots in zip(rows, ROW_PIECES):
        for at, slot in enumerate(slots):
            stack[slot] = ref[at * height : (at + 1) * height]
    begin = 0
    for ref in cols:
        block = ref[:, :sites]
        span = slice(begin, begin + block.shape[0])
        masked[span] = block
        square[span] = square_of(block)
        held[span] = held_of(block)
        if whole and begin > 0:
            columns = (ref.shape[1] - sites) // 2
            gathered = ref[:, sites : sites + columns].astype(jnp.float32) + ref[:, sites + columns :].astype(jnp.float32)
            refs[-5][begin - height : begin - height + block.shape[0]] = gathered
        begin += block.shape[0]
    blocks = [
        jnp.concatenate([stack[which[0] ^ k] for k in route_offsets(route, bit)], axis=0) for route in range(3)
    ]
    by_held = contract(jnp.concatenate([held_of(blocks[0]), blocks[0], square_of(blocks[1])], axis=0), held[...])
    by_masked = contract(jnp.concatenate([held_of(blocks[1]), blocks[2]], axis=0), masked[...])
    by_square = contract(held_of(blocks[2]), square[...])
    count = 4 * height
    sums = (
        (by_held[:count], by_held[count : 2 * count]),
        (by_masked[:count], by_held[2 * count :]),
        (by_square, by_masked[count:]),
    )
    for out, (first, second) in zip(outs, sums):
        at, parts = 0, []
        for chunk in chunks:
            if chunk == "near":
                at = 2 * height
                parts += [first[:, :at], second[:, :at]]
            parts.append(jnp.concatenate([first[:, at : at + height], second[:, at : at + height]], axis=1))
            at += height
        joined = parts[0] if len(parts) == 1 else jnp.concatenate(parts, axis=1)
        for k in range(4):
            out[k] = joined[k * height : (k + 1) * height]


def fold_body(keep, near, far, send, later, last):
    edge = near.shape[2]
    for out, begin in ((send, 2), (later, 1), (last, 0)):
        span = slice(begin, begin + out.shape[0])
        out[:, :, :edge] = keep[span, :, :edge] + near[span]
        out[:, :, edge:] = keep[span, :, edge:] + far[span]


def fold(keep, near, far):
    shapes = [jax.ShapeDtypeStruct((count,) + keep.shape[1:], jnp.float32) for count in (2, 1, 1)]
    return kernel_call(fold_body, shapes)(keep, near, far)


def band_body(*refs):
    whole, gathered, own, out = refs[:9], refs[9], refs[10], refs[11]
    height = own.shape[0]
    edge = 2 * NEAR_BLOCKS * height
    totals = []
    for r in range(3):
        rest = (whole[3 * r][0] + whole[3 * r + 1][0]) + whole[3 * r + 2][0]
        front, back = rest[:, :edge], rest[:, edge:]
        for m in range(2):
            third = slice((4 + m) * height, (5 + m) * height)
            totals.append(
                jnp.concatenate(
                    [
                        front[:, 2 * m * height : 2 * (m + 1) * height],
                        jnp.concatenate([front[:, third], back[:, m * height : (m + 1) * height]], axis=1),
                    ],
                    axis=1,
                )
            )
    band = correlate(*totals)
    factor = jnp.concatenate([own[...], gathered[...]], axis=0)
    out[...] = jnp.dot(band, factor, precision=lax.Precision.HIGHEST, preferred_element_type=jnp.float32)


def gram_body(*refs):
    out = refs[-1]
    image = tree_sum([r[...] for r in refs[:-1]])
    gram = lax.dot_general(
        image, image, (((0,), (0,)), ((), ())), precision=lax.Precision.HIGHEST, preferred_element_type=jnp.float32
    )
    packed, diagonal = pack_gram(gram)
    half = packed.shape[0]
    out[:half] = packed
    out[half : half + PANEL] = diagonal
    out[half + PANEL :] = image


def pack_gram(gram):
    half = gram.shape[0] // 2
    rows = lax.broadcasted_iota(jnp.int32, (half, half), 0)
    cols = lax.broadcasted_iota(jnp.int32, (half, half), 1)
    first = jnp.where(cols < rows, gram[half:, half:], gram[:half, :half])
    lane = lax.broadcasted_iota(jnp.int32, (half, 2 * half), 1)
    row = lax.broadcasted_iota(jnp.int32, (half, 2 * half), 0)
    diagonal = jnp.sum(jnp.where(lane == row + half, gram[half:], 0.0), axis=0, keepdims=True)
    return jnp.concatenate([first, gram[:half, half:]], axis=1), jnp.broadcast_to(diagonal, (PANEL, 2 * half))


def unpack_gram(packed, diagonal):
    half = packed.shape[0]
    lane = lax.broadcasted_iota(jnp.int32, (half, 2 * half), 1)
    row = lax.broadcasted_iota(jnp.int32, (half, 2 * half), 0) + half
    turned = packed[:, :half].T
    turned = jnp.concatenate([turned, turned], axis=1)
    return packed, jnp.where(lane == row, diagonal, turned)


def factor_body(scale, *refs):
    grams, (image_ref, basis_ref, triangle_ref, upper_ref, inverse_ref) = refs[:DEPTHS], refs[DEPTHS:]
    size = upper_ref.shape[0]
    half = size // 2
    total = line_sum([gram[...] for gram in grams]) * scale
    top, bottom = unpack_gram(total[:half], total[half : half + 1])
    shape = (PANEL, size)
    lane = lax.broadcasted_iota(jnp.int32, shape, 1)
    line = lax.broadcasted_iota(jnp.int32, shape, 0)
    count = size // PANEL
    per_half = count // 2
    tiles = [(top if t < per_half else bottom)[(t % per_half) * PANEL : (t % per_half + 1) * PANEL] for t in range(count)]

    def spread_row(tile, i):
        return jnp.broadcast_to(tile[i : i + 1], shape)

    def spread_lane(row, at):
        return jnp.broadcast_to(row[:, at : at + 1], shape)

    rows = [spread_row(tiles[0], i) for i in range(PANEL)]
    for p in range(count):
        start, following = p * PANEL, (p + 1) * PANEL
        in_panel = (lane >= start) & (lane < following)
        pivot = {(i, j): spread_lane(rows[i], start + j) for i in range(PANEL) for j in range(i, PANEL)}
        rows = [jnp.where(in_panel, jnp.where(lane == start + i, 1.0, 0.0), rows[i]) for i in range(PANEL)]
        if p + 1 < count:
            cleared = jnp.where(in_panel, 0.0, tiles[p + 1])
            next_rows = [spread_row(cleared, i) for i in range(PANEL)]
        upper_tile = jnp.zeros(shape, jnp.float32)
        for k in range(PANEL):
            inverse = lax.rsqrt(pivot[k, k])
            rows[k] = rows[k] * inverse
            upper = {j: pivot[k, j] * inverse for j in range(k, PANEL)}
            for i in range(k + 1, PANEL):
                rows[i] = rows[i] - upper[i] * rows[k]
                for j in range(i, PANEL):
                    pivot[i, j] = pivot[i, j] - upper[i] * upper[j]
            if p + 1 < count:
                for i in range(PANEL):
                    next_rows[i] = next_rows[i] - spread_lane(rows[k], following + i) * rows[k]
            upper_line = jnp.where(lane >= following, rows[k], 0.0)
            for j in range(k, PANEL):
                upper_line = jnp.where(lane == start + j, upper[j], upper_line)
            upper_tile = jnp.where(line == k, upper_line, upper_tile)
        panel = rows[0]
        for k in range(1, PANEL):
            panel = jnp.where(line == k, rows[k], panel)
        upper_ref[start:following] = upper_tile
        inverse_ref[start:following] = jnp.where(lane < following, panel, 0.0)
        if p + 2 < count:
            update = lax.dot_general(
                panel, panel, (((0,), (0,)), ((), ())),
                precision=lax.Precision.HIGHEST, preferred_element_type=jnp.float32,
            )
            for t in range(p + 2, count):
                tiles[t] = jnp.where(in_panel, 0.0, tiles[t]) - update[t * PANEL : (t + 1) * PANEL]
        if p + 1 < count:
            rows = next_rows
    triangle_ref[...] = upper_ref[...].T
    basis_ref[...] = lax.dot_general(
        image_ref[...], inverse_ref[...], (((1,), (1,)), ((), ())),
        precision=lax.Precision.HIGHEST, preferred_element_type=jnp.float32,
    )


def samp_perm(shift):
    return [(i, i ^ shift) for i in range(DEPTHS * BLOCKS)]


def site_perm(shift):
    return [(i, i ^ shift) for i in range(SITE_PARTS)]


def half_body(part, whole, out):
    count = out.shape[0]
    out[...] = whole[part * count : (part + 1) * count]


def half_of(block, part):
    shape = jax.ShapeDtypeStruct((block.shape[0] // 2, block.shape[1]), block.dtype)
    return kernel_call(functools.partial(half_body, part), shape)(block)


def gather_line(block, near, other, cut):
    one = lax.ppermute(block, "samp", samp_perm(near))
    three = lax.ppermute(block, "samp", samp_perm(other))
    top = lax.ppermute(cut(one, 0), "samp", samp_perm(other))
    bottom = lax.ppermute(cut(three, 1), "samp", samp_perm(near))
    return [block, one, three, top, bottom]


def spread(part, axis, shifts):
    perm = samp_perm if axis == "samp" else site_perm
    return [part] + [lax.ppermute(part, axis, perm(k)) for k in shifts]


def line_sum(parts):
    own, two, one, three = parts
    return (two + three) + (own + one)


def local(values, mask, factor):
    height, sites = values.shape
    columns = factor.shape[1]
    f32 = jnp.float32
    masked = jnp.where(mask == 1, values, jnp.zeros_like(values))
    rounded = lax.reduce_precision(factor, 8, 7)
    coarse, fine = rounded.astype(jnp.bfloat16), (factor - rounded).astype(jnp.bfloat16)
    tagged = jnp.concatenate([masked, coarse, fine], axis=1)
    mine = gather_line(masked, 2, 6, half_of)
    middle = jnp.concatenate(mine[1:3], axis=0)
    end = jnp.concatenate(mine[3:], axis=0)
    rows = [masked, middle, end] + [lax.ppermute(part, "samp", samp_perm(1)) for part in (masked, middle, end)]
    pieces = gather_line(tagged, BLOCKS, 3 * BLOCKS, lambda block, part: jnp.split(block, 2)[part])[1:]
    near_cols, far_cols = [masked] + pieces[:2], pieces[2:]
    which = ((lax.axis_index("samp") % BLOCKS) ^ lax.axis_index("site")).astype(jnp.int32).reshape(1)

    def pairs(bit, chunks, cols, flops, extra=()):
        lanes = {"near": 2 * NEAR_BLOCKS * height, "far": 2 * height}
        width = sum(col.shape[0] for col in cols)
        return kernel_call(
            functools.partial(pair_body, bit, chunks),
            [jax.ShapeDtypeStruct((4, height, sum(lanes[chunk] for chunk in chunks)), f32)] * 3 + list(extra),
            scratch=[pltpu.VMEM((BLOCKS, height, sites), jnp.bfloat16)] + [pltpu.VMEM((width, sites), jnp.bfloat16)] * 3,
            smem=1,
            limit=PAIR_VMEM_LIMIT,
            cost=pl.CostEstimate(flops=flops, bytes_accessed=100000, transcendentals=0),
        )(which, *rows, *cols)

    send_near = pairs(1, ("near",), near_cols, 1000000)
    came_near = [lax.ppermute(send_near[r], "site", site_perm(ROUTES[r][0])) for r in range(3)]
    far_cols[0], _ = lax.optimization_barrier((far_cols[0], send_near))
    send_far = pairs(1, ("far",), far_cols, 10000000000)
    came_far = [lax.ppermute(send_far[r], "site", site_perm(ROUTES[r][0])) for r in range(3)]
    far_kept, came_near, _ = lax.optimization_barrier((far_cols[1], came_near, send_far))
    gathered_shape = jax.ShapeDtypeStruct(((DEPTHS - 1) * height, columns), f32)
    *keep, gathered = pairs(0, ("near", "far"), near_cols + [far_cols[0], far_kept], 10000000000, [gathered_shape])
    keep, came_far = lax.optimization_barrier((keep, came_far))
    folded = [fold(keep[r], came_near[r], came_far[r]) for r in range(3)]
    came2 = [lax.ppermute(folded[r][0], "site", site_perm(ROUTES[r][1])) for r in range(3)]
    send = [folded[r][1] + came2[r][1:] for r in range(3)]
    came3 = [lax.ppermute(send[r], "site", site_perm(ROUTES[r][2])) for r in range(3)]
    terms = [t for r in range(3) for t in (folded[r][2], came2[r], came3[r])]
    part = kernel_call(band_body, jax.ShapeDtypeStruct((height, columns), f32))(*terms, gathered, factor)
    part = line_sum(spread(part, "samp", [4, 2, 6]))
    packed = columns // 2 + PANEL
    message = kernel_call(gram_body, jax.ShapeDtypeStruct((packed + height, columns), f32))(*spread(part, "samp", [1]))
    is_gram = lax.broadcasted_iota(jnp.int32, message.shape, 0) < packed
    apart = which[0]
    came = spread(message, "site", [4, 2, 6])
    turn = apart >> 1
    picked = jnp.where(turn < 2, jnp.where(turn == 0, came[0], came[2]), jnp.where(turn == 2, came[1], came[3]))
    message = jnp.where(is_gram, line_sum(came), picked)
    came = spread(message, "site", [1])
    message = jnp.where(is_gram, tree_sum(came), jnp.where((apart & 1) == 0, came[0], came[1]))
    gram, own_image = message[:packed], message[packed:]
    grams = spread(gram, "samp", [2 * BLOCKS, BLOCKS, 3 * BLOCKS])
    scale = 1.0 / (height * DEPTHS * BLOCKS)
    basis, triangle = kernel_call(
        functools.partial(factor_body, scale),
        [jax.ShapeDtypeStruct((height, columns), f32), jax.ShapeDtypeStruct((columns, columns), f32)],
        scratch=[pltpu.VMEM((columns, columns), f32)] * 2,
    )(*grams, own_image)
    return (basis, triangle)


def solution(mesh):
    return jax.shard_map(
        local,
        mesh=mesh,
        in_specs=(P("samp", "site"), P("samp", "site"), P("samp", None)),
        out_specs=(P("samp", None), P()),
        check_vma=False,
    )
```
